256 devices in a mesh: gx: 32 (over z, x), gy: 8 (over y, core).
Axes of the slice: x: 4, y: 4, z: 8, core: 2. Of those that a mesh axis runs over, the one named last changes fastest.
Arguments:
- start_field: float32 [16, 512, 128, 128], P(None, 'gx', 'gy'), may hold values from -4 to 4
- currents: float32 [256, 16], replicated, may hold values from -6 to 6
- electrode_map: int32 [2, 512, 128], P(None, 'gx', 'gy'), may hold values from 0 to 256, as said below
- contact_gain: float32 [256], replicated, may hold values from 0.5 to 5
- region_label: int32 [512, 128, 128], P('gx', 'gy'), may hold values from 0 to 7
- region_cond: float32 [8], replicated, may hold values from 0.2 to 5
- texture: float32 [512, 128, 128], P('gx', 'gy'), may hold values from 0.5 to 2
Outputs:
- solution_field: float32 [16, 512, 128, 128], P(None, 'gx', 'gy')
- voltages: float32 [16, 256], replicated
The draws below stay inside these ranges and needn't reach their ends.
Inputs may be any that keep to these rules, and one draw needn't show every extreme that they name: `electrode_map`: each of the 256 electrode numbers 1 to 256 covers exactly one square of 2 x 2 voxels aligned to multiples of 2 on one of the two end faces; all other voxels hold 0.
All inputs are finite; a program needn't handle non-finite values.
Results may differ from the reference program's by a relative error of at most 0.0003.
Values sent between devices are 32-bit elements; how exact they have to be, the bound alone decides.
No kernel may reach another device: no remote copies, remote signals or barrier semaphores. Data moves between devices by JAX's collectives and lax.ppermute only.
A program may use at most 128 MiB of HBM per device.

```python
import math
import jax
import jax.numpy as jnp
from jax import lax

PATTERNS = 16
ELECTRODES = 256
REGIONS = 8
PATCH = 2
SWEEPS = 3
ITERS = 2
NX = 512
NY = 128
NZ = 128


def draw_electrode_map(key, part):
    key = jax.random.fold_in(key, 3)
    patch_rows = NX // PATCH
    patch_cols = NY // PATCH
    shuffled = jax.random.permutation(key, 2 * patch_rows * patch_cols)
    labels = jnp.where(shuffled < ELECTRODES, shuffled + 1, 0).astype(jnp.int32)
    labels = labels.reshape(2, patch_rows, patch_cols)
    return jnp.repeat(jnp.repeat(labels, PATCH, axis=1), PATCH, axis=2)


def draw_start_field(key, part):
    key = jax.random.fold_in(key, 11)
    common_key, own_key, weight_key, spread_key, sign_key = jax.random.split(key, 5)
    signs = jnp.where(jax.random.bernoulli(sign_key, 0.5, (PATTERNS,)), 1.0, -1.0).astype(jnp.float32)
    common = jax.random.normal(common_key, (NX, NY, NZ), jnp.float32)
    own = jax.random.normal(own_key, (PATTERNS, NX, NY, NZ), jnp.float32)
    weights = jax.random.uniform(weight_key, (PATTERNS,), jnp.float32, 0.5, 1.0)
    spread = jax.random.uniform(spread_key, (PATTERNS,), jnp.float32, 0.6, 1.0)
    field = (signs * weights)[:, None, None, None] * common[None] + spread[:, None, None, None] * own
    return jnp.clip(field, -4.0, 4.0).astype(jnp.float32)


def plant(result, key, low, top_value):
    longest = result.shape.index(max(result.shape))
    spots = []
    for shift in (0, 1):
        where = [jax.random.randint(jax.random.fold_in(key, axis), (), 0, length) for axis, length in enumerate(result.shape)]
        where[longest] = (where[longest] + shift) % result.shape[longest]
        spots.append(tuple(where))
    return result.at[spots[0]].set(low).at[spots[1]].set(top_value)


def level_of(stream_key, extent, pieces, smallest, high):
    def one(axis_at, shards_of):
        draws = jax.random.uniform(jax.random.fold_in(jax.random.fold_in(stream_key, 6), axis_at), (shards_of,), jnp.float32, smallest / len(pieces), high / len(pieces))
        return jnp.repeat(jnp.exp(draws), extent[axis_at] // shards_of).reshape((-1,) + (1,) * (len(extent) - axis_at - 1))

    factor_of = one(*pieces[0])
    for cut in pieces[1:]:
        factor_of = factor_of * one(*cut)
    return factor_of


def bell_draw(key, shape, width, bound, kind=jnp.bfloat16):
    array = jax.random.normal(key, shape, jnp.float32) * width
    return jnp.minimum(jnp.maximum(array, -bound), bound).astype(kind)


def setup_inputs(seed: int = 0) -> dict:
    streams_of = jax.random.split(jax.random.key(seed), 8)
    start_field = draw_start_field(jax.random.fold_in(streams_of[7], 71), 0)
    currents = bell_draw(streams_of[1], (ELECTRODES, PATTERNS), 1.0, 6.0, jnp.float32)
    electrode_map = draw_electrode_map(jax.random.fold_in(streams_of[7], 71), 0)
    contact_gain = jnp.clip(jnp.exp(jax.random.uniform(streams_of[3], (ELECTRODES,), jnp.float32, math.log(0.5), math.log(5.0))), 0.5, 5.0)
    region_label = plant(jax.random.randint(streams_of[4], (NX, NY, NZ), 0, REGIONS), jax.random.fold_in(streams_of[4], 1), 0, REGIONS - 1).astype(jnp.int32)
    region_cond = jnp.clip(jnp.exp(jax.random.uniform(streams_of[5], (REGIONS,), jnp.float32, math.log(0.2), math.log(5.0))), 0.2, 5.0)
    texture = jnp.clip(jnp.exp(math.log(2.0) - 1.3862944 * jax.random.uniform(streams_of[6], (NX, NY, NZ), jnp.float32) ** level_of(streams_of[6], (NX, NY, NZ), ((0, 32), (1, 8)), -0.2, 0.2)), 0.5, 2.0)
    return dict(start_field=start_field, currents=currents, electrode_map=electrode_map, contact_gain=contact_gain, region_label=region_label, region_cond=region_cond, texture=texture)


CHEB_LOW = 0.1
CHEB_HIGH = 2.0

def harmonic(own_cond, nbr_cond):
    summed = own_cond + nbr_cond
    divisor = jnp.where(summed > 0, summed, 1.0)
    return 2.0 * own_cond * nbr_cond / divisor

def electrode_onehot(electrode_map):
    numbers = jnp.arange(1, ELECTRODES + 1, dtype=jnp.int32)
    return (electrode_map[..., None] == numbers).astype(jnp.float32)

def region_conductivity(region_label, region_cond, texture):
    numbers = jnp.arange(REGIONS, dtype=jnp.int32)
    onehot = (region_label[..., None] == numbers).astype(jnp.float32)
    return jnp.sum(onehot * region_cond, axis=-1) * texture

def place_ends(lower_face, upper_face, z_cells):
    zindex = lax.broadcasted_iota(jnp.int32, lower_face.shape + (z_cells,), lower_face.ndim)
    return jnp.where(zindex == 0, lower_face[..., None], 0.0) + jnp.where(zindex == z_cells - 1, upper_face[..., None], 0.0)

def coefficients(widened, contact_diag):
    centre = widened[1:-1, 1:-1]
    deep_pad = jnp.pad(centre, ((0, 0), (0, 0), (1, 1)))
    lower_x = harmonic(centre, widened[:-2, 1:-1])
    upper_x = harmonic(centre, widened[2:, 1:-1])
    lower_y = harmonic(centre, widened[1:-1, :-2])
    upper_y = harmonic(centre, widened[1:-1, 2:])
    lower_z = harmonic(centre, deep_pad[:, :, :-2])
    upper_z = harmonic(centre, deep_pad[:, :, 2:])
    diagonal = contact_diag + lower_x + upper_x + lower_y + upper_y + lower_z + upper_z
    positive = diagonal > 0
    inverse = jnp.where(positive, 1.0 / jnp.where(positive, diagonal, 1.0), 0.0)
    return ((lower_x, upper_x, lower_y, upper_y, lower_z, upper_z, contact_diag), inverse)

def pad_sides(values):
    return jnp.pad(values, ((0, 0), (1, 1), (1, 1), (0, 0)))

def stencil(padded, couplings):
    lower_x, upper_x, lower_y, upper_y, lower_z, upper_z, contact_diag = couplings
    centre = padded[:, 1:-1, 1:-1]
    deep_pad = jnp.pad(centre, ((0, 0), (0, 0), (0, 0), (1, 1)))
    return contact_diag * centre + lower_x * (centre - padded[:, :-2, 1:-1]) + upper_x * (centre - padded[:, 2:, 1:-1]) + lower_y * (centre - padded[:, 1:-1, :-2]) + upper_y * (centre - padded[:, 1:-1, 2:]) + lower_z * (centre - deep_pad[..., :-2]) + upper_z * (centre - deep_pad[..., 2:])

def chebyshev(residual, operate_fn, inverse):
    middle = 0.5 * (CHEB_HIGH + CHEB_LOW)
    radius = 0.5 * (CHEB_HIGH - CHEB_LOW)
    sharpness = middle / radius
    rho_now = 1.0 / sharpness
    update = inverse * residual / middle
    iterate = update
    for sweep_index in range(SWEEPS):
        defect = inverse * (residual - operate_fn(iterate))
        rho_next = 1.0 / (2.0 * sharpness - rho_now)
        update = rho_next * rho_now * update + 2.0 * rho_next / radius * defect
        iterate = iterate + update
        rho_now = rho_next
    return iterate

def gram_matrix(first_set, second_set):
    return jnp.einsum('pxyz,qxyz->pq', first_set, second_set, precision=lax.Precision.HIGHEST)

def combine(vectors, mixing):
    return jnp.einsum('pxyz,pq->qxyz', vectors, mixing, precision=lax.Precision.HIGHEST)

def reference(start_field, currents, electrode_map, contact_gain, region_label, region_cond, texture):
    onehot_faces = electrode_onehot(electrode_map)
    contact_faces = jnp.einsum('fxye,e->fxy', onehot_faces, contact_gain, precision=lax.Precision.HIGHEST)
    contact_diag = place_ends(contact_faces[0], contact_faces[1], NZ)
    source_faces = jnp.einsum('fxye,ep->pfxy', onehot_faces, currents, precision=lax.Precision.HIGHEST)
    source = place_ends(source_faces[:, 0], source_faces[:, 1], NZ)
    conduct = region_conductivity(region_label, region_cond, texture)
    widened = jnp.pad(conduct, ((1, 1), (1, 1), (0, 0)))
    couplings, inverse = coefficients(widened, contact_diag)

    def local_apply(values):
        return stencil(pad_sides(values), couplings)

    def operate(fields):
        return lax.map(lambda column: local_apply(column[None])[0], fields)

    def smooth(fields):
        return lax.map(lambda column: chebyshev(column[None], local_apply, inverse)[0], fields)
    solution = start_field
    residual = source - operate(start_field)
    direction = residual
    mapped = residual
    factor = jnp.eye(PATTERNS, dtype=jnp.float32)
    for iter_index in range(ITERS):
        smoothed = smooth(residual)
        if iter_index == 0:
            direction = smoothed
        else:
            cross_terms = gram_matrix(mapped, smoothed)
            beta_coef = -jax.scipy.linalg.cho_solve((factor, True), cross_terms)
            direction = smoothed + combine(direction, beta_coef)
        mapped = operate(direction)
        curvature = gram_matrix(direction, mapped)
        curvature = 0.5 * (curvature + curvature.T)
        projected = gram_matrix(direction, residual)
        factor = jnp.linalg.cholesky(curvature)
        alpha_coef = jax.scipy.linalg.cho_solve((factor, True), projected)
        solution = solution + combine(direction, alpha_coef)
        if iter_index + 1 < ITERS:
            residual = residual - combine(mapped, alpha_coef)
    surface = jnp.stack((solution[..., 0], solution[..., NZ - 1]), axis=1)
    face_sums = jnp.einsum('fxye,pfxy->pe', onehot_faces, surface, precision=lax.Precision.HIGHEST)
    return (solution, face_sums / (PATCH * PATCH))
```

```python
import functools

import jax
import jax.numpy as jnp
import numpy as np
from jax import lax
from jax.experimental import pallas as pl
from jax.experimental.pallas import tpu as pltpu
from jax.sharding import PartitionSpec as P

ELECTRODES = 256
REGIONS = 8
PATCH = 2
SWEEPS = 3
CHEB_LOW = 0.1
CHEB_HIGH = 2.0

PATS = 16
BLK = 16
NZ = 128
DEEP = 9
EXT = BLK + 2 * DEEP
ROWS = 3 * BLK
YOFF = BLK - DEEP
COND = BLK
FACE = BLK + 1
UPPER = 64
CONTACT = 32

F32 = jnp.float32
BF16 = jnp.bfloat16
HIGHEST = lax.Precision.HIGHEST


def polynomial():
    middle = 0.5 * (CHEB_HIGH + CHEB_LOW)
    radius = 0.5 * (CHEB_HIGH - CHEB_LOW)
    sharp = middle / radius
    rho = 1.0 / sharp
    step = np.array([1.0])
    n_of_s = np.array([1.0, -1.0])
    update = np.array([1.0 / middle])
    iterate = update
    for _ in range(SWEEPS):
        defect = np.polynomial.polynomial.polysub(
            step, np.polynomial.polynomial.polymul(n_of_s, iterate)
        )
        rho_next = 1.0 / (2.0 * sharp - rho)
        update = np.polynomial.polynomial.polyadd(
            rho_next * rho * update, 2.0 * rho_next / radius * defect
        )
        iterate = np.polynomial.polynomial.polyadd(iterate, update)
        rho = rho_next
    return [float(v) for v in iterate]


E0, E1, E2, E3 = polynomial()
MIX = (E2 / E3, E1 / E3, E0 / E3)


def corner_blocks():
    rows = [(0, i, DEEP - i) for i in range(1, DEEP)]
    rows += [(1, i, i + 1) for i in range(DEEP - 1)]
    return rows


CORNER = sum(DEEP - k for _, _, k in corner_blocks()) + 2 * len(corner_blocks())


def vmem(mib):
    return pltpu.CompilerParams(vmem_limit_bytes=mib * 1024 * 1024)


VM = pl.BlockSpec(memory_space=pltpu.VMEM)
SM = pl.BlockSpec(memory_space=pltpu.SMEM)


def pack_kernel(side, cond, start, label, texture, face, block, up, down, mate, away):
    side_c = side[0]

    def row(x, carry):
        block[x, 0:BLK] = pltpu.einshape("pyz->ypz", start[:, x])
        lab = label[x]
        value = jnp.zeros((BLK, NZ), F32)
        for region in range(REGIONS):
            value = jnp.where(lab == region, cond[region], value)
        block[x, COND] = value * texture[x]
        block[x, FACE] = face[x]
        return carry

    lax.fori_loop(0, BLK, row, 0)
    base_mate = (BLK - DEEP) * (1 - side_c)
    base_away = (BLK - DEEP) * side_c

    def faces(x, carry):
        for j in range(DEEP):
            mate[x, j] = block[x, base_mate + j]
            away[x, j] = block[x, base_away + j]
        for j in range(2):
            mate[x, DEEP + j] = block[x, COND + j]
            away[x, DEEP + j] = block[x, COND + j]
        return carry

    lax.fori_loop(0, BLK, faces, 0)

    def ends(x, carry):
        for j in range(BLK + 2):
            up[x, j] = block[BLK - DEEP + x, j]
            down[x, j] = block[x, j]
        return carry

    lax.fori_loop(0, DEEP, ends, 0)


def pack(side, region_cond, start, label, texture, face):
    shape = jax.ShapeDtypeStruct
    return pl.pallas_call(
        pack_kernel,
        out_shape=(
            shape((BLK, BLK + 2, PATS, NZ), F32),
            shape((DEEP, BLK + 2, PATS, NZ), F32),
            shape((DEEP, BLK + 2, PATS, NZ), F32),
            shape((BLK, DEEP + 2, PATS, NZ), F32),
            shape((BLK, DEEP + 2, PATS, NZ), F32),
        ),
        in_specs=[SM, SM, VM, VM, VM, VM],
        out_specs=(VM,) * 5,
        compiler_params=vmem(40),
    )(side, region_cond, start, label, texture, face)


def corner_kernel(side, low, high, mate, away):
    side_c = side[0]
    at = 0
    for which, i, k in corner_blocks():
        src = low if which == 0 else high
        count = DEEP - k
        base_mate = (BLK - count) * (1 - side_c)
        base_away = (BLK - count) * side_c
        for j in range(count):
            mate[at] = src[i, base_mate + j]
            away[at] = src[i, base_away + j]
            at += 1
        for j in range(2):
            mate[at] = src[i, COND + j]
            away[at] = src[i, COND + j]
            at += 1


def corners(side, low, high):
    shape = jax.ShapeDtypeStruct((CORNER, PATS, NZ), F32)
    return pl.pallas_call(
        corner_kernel,
        out_shape=(shape, shape),
        in_specs=[SM, VM, VM],
        out_specs=(VM, VM),
        compiler_params=vmem(24),
    )(side, low, high)


def harmonic(own, other):
    total = own + other
    return 2.0 * own * other / jnp.where(total > 0, total, 1.0)


def split(value):
    high = value.astype(BF16)
    return high, (value - high.astype(F32)).astype(BF16)


def split3(value):
    high = value.astype(BF16)
    rest = value - high.astype(F32)
    middle = rest.astype(BF16)
    return high, middle, (rest - middle.astype(F32)).astype(BF16)


def gram(first, seconds, origin):
    width = 2 * PATS * len(seconds)

    def row(i, total):
        x = origin + i

        def flat(ref):
            return jnp.concatenate([ref[x, origin + j] for j in range(BLK)], axis=1)

        left = jnp.concatenate(split(flat(first)), axis=0)
        parts = [split(flat(ref)) for ref in seconds]
        right = jnp.concatenate([p[0] for p in parts] + [p[1] for p in parts], axis=0)
        return total + lax.dot_general(
            left, right, (((1,), (1,)), ((), ())), preferred_element_type=F32
        )

    total = lax.fori_loop(0, BLK, row, jnp.zeros((2 * PATS, width), F32))
    total = total[:PATS] + total[PATS:]
    half = width // 2
    return total[:, :half] + total[:, half:]


def main_kernel(
    side, marks, block, low, high, mate, away, cmate, caway,
    out_u, out_z, out_scale, out_chunk,
    fa, fb, fc, faces, cond, cx, cy, cz, diag, scale, volt,
):
    side_c = side[0]
    lane = lax.broadcasted_iota(jnp.int32, (PATS, NZ), 1)
    first_lane = lane == 0
    last_lane = lane == NZ - 1

    zero = jnp.zeros((PATS, NZ), F32)

    def clear(i, carry):
        for j in range(DEEP):
            fa[i, j] = zero
            fa[i, EXT - 1 - j] = zero
            fa[EXT - 1 - i, j] = zero
            fa[EXT - 1 - i, EXT - 1 - j] = zero
        return carry

    lax.fori_loop(0, DEEP, clear, 0)
    for which in (0, 2):
        for i in (0, EXT - 1):
            faces[i, which] = zero
            cond[i, which * BLK : (which + 1) * BLK] = zero

    def put_row(dst, src, x):
        for j in range(BLK):
            fa[dst, DEEP + j] = src[x, j]
        cond[dst, BLK : 2 * BLK] = src[x, COND]
        faces[dst, 1] = src[x, FACE]

    def own_rows(x, carry):
        put_row(DEEP + x, block, x)
        return carry

    def halo_rows(x, carry):
        put_row(x, low, x)
        put_row(DEEP + BLK + x, high, x)
        return carry

    lax.fori_loop(0, BLK, own_rows, 0)
    lax.fori_loop(0, DEEP, halo_rows, 0)

    def put_sides(below, above, cbelow, cabove):
        def side_rows(x, carry):
            for j in range(DEEP):
                fa[DEEP + x, j] = below[x, j]
                fa[DEEP + x, DEEP + BLK + j] = above[x, j]
            for src, which in ((below, 0), (above, 2)):
                cond[DEEP + x, which * BLK : (which + 1) * BLK] = src[x, DEEP]
                faces[DEEP + x, which] = src[x, DEEP + 1]
            return carry

        lax.fori_loop(0, BLK, side_rows, 0)
        at = 0
        for which_x, i, k in corner_blocks():
            x = i if which_x == 0 else DEEP + BLK + i
            for j in range(DEEP - k):
                fa[x, k + j] = cbelow[at]
                fa[x, DEEP + BLK + j] = cabove[at]
                at += 1
            for src, which in ((cbelow, 0), (cabove, 2)):
                cond[x, which * BLK : (which + 1) * BLK] = src[at]
                faces[x, which] = src[at + 1]
            at += 2

    @pl.when(side_c == 0)
    def _():
        put_sides(away, mate, caway, cmate)

    @pl.when(side_c == 1)
    def _():
        put_sides(mate, away, cmate, caway)

    wide_lane = lax.broadcasted_iota(jnp.int32, (ROWS, NZ), 1)

    def conductances(x, carry):
        here = cond[x]
        cx[x] = harmonic(here, cond[jnp.minimum(x + 1, EXT - 1)])
        cy[x] = harmonic(here, pltpu.roll(here, ROWS - 1, 0))
        cz[x] = jnp.where(
            wide_lane == NZ - 1, 0.0, harmonic(here, pltpu.roll(here, NZ - 1, 1))
        )
        return carry

    lax.fori_loop(0, EXT, conductances, 0)

    def diagonals(x, carry):
        face = jnp.concatenate([faces[x, 0], faces[x, 1], faces[x, 2]], axis=0)
        contact = jnp.where(
            wide_lane == 0,
            pltpu.roll(face, NZ - CONTACT, 1),
            jnp.where(
                wide_lane == NZ - 1, pltpu.roll(face, NZ - 2 - CONTACT, 1), 0.0
            ),
        )
        own_y = cy[x]
        own_z = cz[x]
        total = (
            contact
            + cx[x]
            + cx[jnp.maximum(x - 1, 0)]
            + own_y
            + pltpu.roll(own_y, 1, 0)
            + own_z
            + pltpu.roll(own_z, 1, 1)
        )
        positive = total > 0
        diag[x] = total
        scale[x] = jnp.where(positive, lax.rsqrt(jnp.where(positive, total, 1.0)), 0.0)
        return carry

    lax.fori_loop(0, EXT, diagonals, 0)

    def at_row(ref, x, y):
        return ref[x, pl.ds(y + YOFF, 1), :]

    def neighbours(src, x, y, below, here, above):
        weight = at_row(cz, x, y)
        return (
            at_row(cx, x - 1, y) * src[x - 1, y]
            + at_row(cx, x, y) * src[x + 1, y]
            + at_row(cy, x, y - 1) * below
            + at_row(cy, x, y) * above
            + weight * pltpu.roll(here, NZ - 1, 1)
            + pltpu.roll(weight * here, 1, 1)
        )

    def sweep(radius, src, finish):
        lo, hi = DEEP - radius, DEEP + BLK + radius

        def row(x, carry):
            below, here = src[x, lo - 1], src[x, lo]
            for y in range(lo, hi):
                above = src[x, y + 1]
                finish(x, y, here, neighbours(src, x, y, below, here, above))
                below, here = here, above
            return carry

        lax.fori_loop(lo, hi, row, 0)

    def residual(x, y, here, total):
        which, spot = (
            (0, y + YOFF) if y < DEEP
            else (1, y - DEEP) if y < DEEP + BLK
            else (2, y - DEEP - BLK)
        )
        face = faces[x, which]
        source = jnp.where(
            first_lane,
            pltpu.roll(face, (NZ - spot) % NZ, 1),
            jnp.where(last_lane, pltpu.roll(face, NZ - 1 - UPPER - spot, 1), 0.0),
        )
        fb[x, y] = at_row(scale, x, y) * (source - at_row(diag, x, y) * here + total)

    sweep(DEEP - 1, fa, residual)

    def rescale(x, carry):
        here = scale[x]
        cx[x] = cx[x] * here * scale[jnp.minimum(x + 1, EXT - 1)]
        cy[x] = cy[x] * here * pltpu.roll(here, ROWS - 1, 0)
        cz[x] = cz[x] * here * pltpu.roll(here, NZ - 1, 1)
        return carry

    lax.fori_loop(0, EXT, rescale, 0)

    def mixed(dst, base, factor):
        def finish(x, y, here, total):
            dst[x, y] = factor * base[x, y] + total

        return finish

    def mapped(dst):
        def finish(x, y, here, total):
            dst[x, y] = here - total

        return finish

    def smooth(radius, base, one, two):
        sweep(radius + 2, base, mixed(one, base, MIX[0]))
        sweep(radius + 1, one, mixed(two, base, MIX[1]))
        sweep(radius, two, mixed(one, base, MIX[2]))

    smooth(5, fb, fa, fc)
    sweep(4, fa, mapped(fc))
    gram_first = gram(fa, (fb, fc), DEEP)

    def save(dst, src):
        def row(x, carry):
            for y in range(BLK):
                dst[x, y] = src[DEEP + x, DEEP + y]
            return carry

        lax.fori_loop(0, BLK, row, 0)

    save(out_u, fa)
    smooth(1, fc, fb, fa)
    sweep(0, fb, mapped(fa))
    gram_second = gram(fb, (fc, fa), DEEP)
    save(out_z, fb)

    def save_scale(x, carry):
        out_scale[x] = scale[DEEP + x, BLK : 2 * BLK]
        return carry

    lax.fori_loop(0, BLK, save_scale, 0)

    volt[...] = jnp.zeros_like(volt)
    elane = lax.broadcasted_iota(jnp.int32, (PATS, ELECTRODES), 1)
    half = BLK // PATCH

    def electrode(i, carry):
        mark = marks[i]

        @pl.when(mark > 0)
        def _():
            face = i // (half * half)
            x0 = (i // half) % half * PATCH
            y0 = i % half * PATCH
            wanted = lane == face * (NZ - 1)
            sums = [zero, zero, zero]
            for dx in range(PATCH):
                for dy in range(PATCH):
                    x, y = x0 + dx, y0 + dy
                    weight = out_scale[x, pl.ds(y, 1), :]
                    sums[0] += block[x, y]
                    sums[1] += weight * out_u[x, y]
                    sums[2] += weight * out_z[x, y]
            for f in range(3):
                total = jnp.sum(jnp.where(wanted, sums[f], 0.0), axis=1, keepdims=True)
                volt[f] = volt[f] + jnp.where(elane == mark - 1, total, 0.0)

        return carry

    lax.fori_loop(0, 2 * half * half, electrode, 0)

    grams = jnp.concatenate(
        [gram_first, gram_second, jnp.zeros((PATS, NZ - 4 * PATS), F32)], axis=1
    )
    per = ELECTRODES // 8
    for d in range(8):
        tile, spot = d * per // NZ, d * per % NZ
        picked = zero
        for f in range(3):
            part = volt[f, :, tile * NZ : (tile + 1) * NZ]
            part = pltpu.roll(part, (per * f - spot) % NZ, 1)
            inside = (lane >= per * f) & (lane < per * (f + 1))
            picked = jnp.where(inside, part, picked)
        out_chunk[d, 0:PATS] = picked
        out_chunk[d, PATS : 2 * PATS] = grams


def main_call(side, marks, block, low, high, mate, away, cmate, caway):
    shape = jax.ShapeDtypeStruct
    field = pltpu.VMEM((EXT, EXT, PATS, NZ), F32)
    plane = pltpu.VMEM((EXT, ROWS, NZ), F32)
    return pl.pallas_call(
        main_kernel,
        out_shape=(
            shape((BLK, BLK, PATS, NZ), F32),
            shape((BLK, BLK, PATS, NZ), F32),
            shape((BLK, BLK, NZ), F32),
            shape((8, 2 * PATS, NZ), F32),
        ),
        in_specs=[SM, SM] + [VM] * 7,
        out_specs=(VM,) * 4,
        scratch_shapes=[
            field, field, field,
            pltpu.VMEM((EXT, 3, PATS, NZ), F32),
            plane, plane, plane, plane, plane, plane,
            pltpu.VMEM((3, PATS, ELECTRODES), F32),
        ],
        compiler_params=vmem(60),
    )(side, marks, block, low, high, mate, away, cmate, caway)


def solve_kernel(parts, out_mix, out_volt):
    volts = parts[0, 0:PATS]
    grams = parts[0, PATS : 2 * PATS]
    for i in range(1, parts.shape[0]):
        volts = volts + parts[i, 0:PATS]
        grams = grams + parts[i, PATS : 2 * PATS]
    lane = lax.broadcasted_iota(jnp.int32, (PATS, NZ), 1)

    a_at, b_at, c_at, e_at = 0, PATS, 2 * PATS, 3 * PATS

    def move(source, target):
        return pltpu.roll(grams, (target - source) % NZ, 1)

    def pick(first, second, third):
        return jnp.where(
            lane < PATS,
            move(first, 0),
            jnp.where(
                lane < 2 * PATS,
                move(second, PATS),
                jnp.where(lane < 3 * PATS, move(third, 2 * PATS), 0.0),
            ),
        )

    table = jnp.concatenate([pick(b_at, c_at, a_at), pick(c_at, e_at, b_at)], axis=0)
    rows = lax.broadcasted_iota(jnp.int32, (2 * PATS, NZ), 0)
    for k in range(2 * PATS):
        pivot = table[k : k + 1] / table[k : k + 1, k : k + 1]
        table = jnp.where(rows == k, pivot, table - table[:, k : k + 1] * pivot)
    mix = table[:, 2 * PATS : 3 * PATS]
    eye = (
        lax.broadcasted_iota(jnp.int32, (PATS, PATS), 0)
        == lax.broadcasted_iota(jnp.int32, (PATS, PATS), 1)
    ).astype(F32)
    turned = lax.dot_general(
        eye, mix, (((1,), (1,)), ((), ())), precision=HIGHEST, preferred_element_type=F32
    )
    out_mix[...] = turned
    per = ELECTRODES // 8
    fields = jnp.concatenate(
        [pltpu.roll(volts, NZ - per, 1), pltpu.roll(volts, NZ - 2 * per, 1)], axis=0
    )
    total = volts + jnp.dot(turned, fields, precision=HIGHEST, preferred_element_type=F32)
    out_volt[...] = total * (1.0 / (PATCH * PATCH))


def solve_small(parts):
    shape = jax.ShapeDtypeStruct
    return pl.pallas_call(
        solve_kernel,
        out_shape=(shape((PATS, 2 * PATS), F32), shape((PATS, NZ), F32)),
        in_specs=[VM],
        out_specs=(VM, VM),
        compiler_params=vmem(16),
    )(parts)


def update_kernel(mix, start, u, z, scale, out):
    left = jnp.concatenate(
        [jnp.concatenate([part] * 3, axis=1) for part in split3(mix[...])], axis=0
    )

    def row(x, carry):
        data = jnp.concatenate(
            [
                jnp.concatenate([u[x, y] for y in range(BLK)], axis=1),
                jnp.concatenate([z[x, y] for y in range(BLK)], axis=1),
            ],
            axis=0,
        )
        right = jnp.concatenate(split3(data), axis=0)
        both = jnp.dot(left, right, preferred_element_type=F32)
        both = both[:PATS] + (both[PATS : 2 * PATS] + both[2 * PATS :])
        change = jnp.stack(
            [
                both[:, y * NZ : (y + 1) * NZ] * scale[x, pl.ds(y, 1), :]
                for y in range(BLK)
            ],
            axis=0,
        )
        out[:, x] = start[:, x] + pltpu.einshape("ypz->pyz", change)
        return carry

    lax.fori_loop(0, BLK, row, 0)


def update(mix, start, u, z, scale):
    return pl.pallas_call(
        update_kernel,
        out_shape=jax.ShapeDtypeStruct(start.shape, F32),
        in_specs=[VM] * 5,
        out_specs=VM,
        compiler_params=vmem(24),
    )(mix, start, u, z, scale)


def face_blocks(electrode_map, currents, contact_gain):
    numbers = jnp.arange(1, ELECTRODES + 1, dtype=jnp.int32)
    onehot = (electrode_map[..., None] == numbers).astype(F32)
    contact = jnp.einsum("fxye,e->xyf", onehot, contact_gain, precision=HIGHEST)
    source = jnp.einsum("fxye,ep->fxpy", onehot, currents, precision=HIGHEST)
    gap = lambda width: jnp.zeros((BLK, PATS, width), F32)
    return jnp.concatenate(
        [
            source[0], gap(CONTACT - BLK), contact, gap(UPPER - CONTACT - 2),
            source[1], gap(NZ - UPPER - BLK),
        ],
        axis=2,
    )


def body(start_field, currents, electrode_map, contact_gain, region_label, region_cond, texture):
    gx, gy = lax.axis_size("gx"), lax.axis_size("gy")
    side = (lax.axis_index("gy") % 2).astype(jnp.int32).reshape(1)
    marks = electrode_map[:, ::PATCH, ::PATCH].reshape(-1)
    face = face_blocks(electrode_map, currents, contact_gain)
    block, up, down, mate, away = pack(
        side, region_cond, start_field, region_label, texture, face
    )
    rise = [(i, i + 1) for i in range(gx - 1)]
    fall = [(j, i) for i, j in rise]
    pairs = [(i, i + 1) for i in range(0, gy, 2)]
    gaps = [(i, i + 1) for i in range(1, gy - 1, 2)]
    within = pairs + [(j, i) for i, j in pairs]
    across = gaps + [(j, i) for i, j in gaps]
    low = lax.ppermute(up, "gx", rise)
    high = lax.ppermute(down, "gx", fall)
    away = lax.ppermute(away, "gy", across)
    mate = lax.ppermute(mate, "gy", within)
    cmate, caway = corners(side, low, high)
    caway = lax.ppermute(caway, "gy", across)
    cmate = lax.ppermute(cmate, "gy", within)
    u, z, scale, chunk = main_call(
        side, marks, block, low, high, mate, away, cmate, caway
    )
    chunk = lax.all_to_all(chunk, "gy", 0, 0, tiled=True)
    chunk = jnp.sum(chunk, axis=0)
    parts = jnp.broadcast_to(chunk[None], (gx,) + chunk.shape)
    parts = lax.all_to_all(parts, "gx", 0, 0, tiled=True)
    mix, volt = solve_small(parts)
    volts = jnp.broadcast_to(volt[None], (gy,) + volt.shape)
    volts = lax.all_to_all(volts, "gy", 0, 0, tiled=True)
    result = update(mix, start_field, u, z, scale)
    per = ELECTRODES // gy
    voltages = volts[:, :, :per].transpose(1, 0, 2).reshape(PATS, ELECTRODES)
    return result, voltages


def solution(mesh):
    placed = (
        P(None, "gx", "gy", None),
        P(),
        P(None, "gx", "gy"),
        P(),
        P("gx", "gy", None),
        P(),
        P("gx", "gy", None),
    )
    return jax.shard_map(
        body,
        mesh=mesh,
        in_specs=placed,
        out_specs=(P(None, "gx", "gy", None), P()),
        check_vma=False,
    )
```

```python
import functools

import jax
import jax.numpy as jnp
import numpy as np
from jax import lax
from jax.experimental import pallas as pl
from jax.experimental.pallas import tpu as pltpu
from jax.sharding import Mesh, PartitionSpec as P

ELECTRODES = 256
REGIONS = 8
PATCH = 2
SWEEPS = 3
CHEB_LOW = 0.1
CHEB_HIGH = 2.0

GX = ("z", "x")
GY = ("y", "c")
PATS = 16
BLK = 16
NZ = 128
DEEP = 9
EXT = BLK + 2 * DEEP
ROWS = 3 * BLK
YOFF = BLK - DEEP
COND = BLK
FACE = BLK + 1
UPPER = 64
CONTACT = 32
MARK = 34
MARKROWS = 40

F32 = jnp.float32
BF16 = jnp.bfloat16
HIGHEST = lax.Precision.HIGHEST


def polynomial():
    middle = 0.5 * (CHEB_HIGH + CHEB_LOW)
    radius = 0.5 * (CHEB_HIGH - CHEB_LOW)
    sharp = middle / radius
    rho = 1.0 / sharp
    step = np.array([1.0])
    n_of_s = np.array([1.0, -1.0])
    update = np.array([1.0 / middle])
    iterate = update
    for _ in range(SWEEPS):
        defect = np.polynomial.polynomial.polysub(
            step, np.polynomial.polynomial.polymul(n_of_s, iterate)
        )
        rho_next = 1.0 / (2.0 * sharp - rho)
        update = np.polynomial.polynomial.polyadd(
            rho_next * rho * update, 2.0 * rho_next / radius * defect
        )
        iterate = np.polynomial.polynomial.polyadd(iterate, update)
        rho = rho_next
    return [float(v) for v in iterate]


E0, E1, E2, E3 = polynomial()
MIX = (E2 / E3, E1 / E3, E0 / E3)


def corner_blocks():
    rows = [(0, i, DEEP - i) for i in range(1, DEEP)]
    rows += [(1, i, i + 1) for i in range(DEEP - 1)]
    return rows


CORNER = sum(DEEP - k for _, _, k in corner_blocks()) + 2 * len(corner_blocks())


def vmem(mib):
    return pltpu.CompilerParams(vmem_limit_bytes=mib * 1024 * 1024)


VM = pl.BlockSpec(memory_space=pltpu.VMEM)
HB = pl.BlockSpec(memory_space=pltpu.HBM)
SM = pl.BlockSpec(memory_space=pltpu.SMEM)


def pack_kernel(
    side, cond, start, label, texture, face, out, up, down, mate, away, block, sem
):
    side_c = side[0]

    def row(x, carry):
        block[x, 0:BLK] = pltpu.einshape("pyz->ypz", start[:, x])
        lab = label[x]
        value = jnp.zeros((BLK, NZ), F32)
        for region in range(REGIONS):
            value = jnp.where(lab == region, cond[region], value)
        block[x, COND] = value * texture[x]
        block[x, FACE] = face[x]
        return carry

    lax.fori_loop(0, BLK, row, 0)
    copy = pltpu.make_async_copy(block, out, sem)
    copy.start()
    base_mate = (BLK - DEEP) * (1 - side_c)
    base_away = (BLK - DEEP) * side_c

    def faces(x, carry):
        for j in range(DEEP):
            mate[x, j] = block[x, base_mate + j]
            away[x, j] = block[x, base_away + j]
        for j in range(2):
            mate[x, DEEP + j] = block[x, COND + j]
            away[x, DEEP + j] = block[x, COND + j]
        return carry

    lax.fori_loop(0, BLK, faces, 0)

    def ends(x, carry):
        for j in range(BLK + 2):
            up[x, j] = block[BLK - DEEP + x, j]
            down[x, j] = block[x, j]
        return carry

    lax.fori_loop(0, DEEP, ends, 0)
    copy.wait()


def pack(side, region_cond, start, label, texture, face):
    shape = jax.ShapeDtypeStruct
    return pl.pallas_call(
        pack_kernel,
        out_shape=(
            shape((BLK, BLK + 2, PATS, NZ), F32),
            shape((DEEP, BLK + 2, PATS, NZ), F32),
            shape((DEEP, BLK + 2, PATS, NZ), F32),
            shape((BLK, DEEP + 2, PATS, NZ), F32),
            shape((BLK, DEEP + 2, PATS, NZ), F32),
        ),
        in_specs=[SM, SM, VM, VM, VM, VM],
        out_specs=(HB,) + (VM,) * 4,
        scratch_shapes=[
            pltpu.VMEM((BLK, BLK + 2, PATS, NZ), F32),
            pltpu.SemaphoreType.DMA,
        ],
        compiler_params=vmem(40),
    )(side, region_cond, start, label, texture, face)


def corner_kernel(side, low, high, mate, away):
    side_c = side[0]
    at = 0
    for which, i, k in corner_blocks():
        src = low if which == 0 else high
        count = DEEP - k
        base_mate = (BLK - count) * (1 - side_c)
        base_away = (BLK - count) * side_c
        for j in range(count):
            mate[at] = src[i, base_mate + j]
            away[at] = src[i, base_away + j]
            at += 1
        for j in range(2):
            mate[at] = src[i, COND + j]
            away[at] = src[i, COND + j]
            at += 1


def corners(side, low, high):
    shape = jax.ShapeDtypeStruct((CORNER, PATS, NZ), F32)
    return pl.pallas_call(
        corner_kernel,
        out_shape=(shape, shape),
        in_specs=[SM, VM, VM],
        out_specs=(VM, VM),
        compiler_params=vmem(24),
    )(side, low, high)


def harmonic(own, other):
    total = own + other
    return 2.0 * own * other / jnp.where(total > 0, total, 1.0)


def split(value):
    high = value.astype(BF16)
    return high, (value - high.astype(F32)).astype(BF16)


def split3(value):
    high = value.astype(BF16)
    rest = value - high.astype(F32)
    middle = rest.astype(BF16)
    return high, middle, (rest - middle.astype(F32)).astype(BF16)


def gram(first, seconds, origin):
    width = 2 * PATS * len(seconds)

    def row(i, total):
        x = origin + i

        def flat(ref):
            return jnp.concatenate([ref[x, origin + j] for j in range(BLK)], axis=1)

        left = jnp.concatenate(split(flat(first)), axis=0)
        parts = [split(flat(ref)) for ref in seconds]
        right = jnp.concatenate([p[0] for p in parts] + [p[1] for p in parts], axis=0)
        return total + lax.dot_general(
            left, right, (((1,), (1,)), ((), ())), preferred_element_type=F32
        )

    total = lax.fori_loop(0, BLK, row, jnp.zeros((2 * PATS, width), F32))
    total = total[:PATS] + total[PATS:]
    half = width // 2
    return total[:, :half] + total[:, half:]


def main_kernel(
    side, marks, block, low, high, mate, away, cmate, caway,
    out_u, out_z, out_scale, out_chunk,
    own, ub, fa, fb, fc, za, zb, faces, cond, cx, cy, cz, diag, scale, volt,
    marked, marked_s, sem, in_sems, out_sems,
):
    side_c = side[0]
    lane = lax.broadcasted_iota(jnp.int32, (PATS, NZ), 1)
    first_lane = lane == 0
    last_lane = lane == NZ - 1

    zero = jnp.zeros((PATS, NZ), F32)
    mid = pl.ds(DEEP, BLK)
    above_mate = 1 - side_c
    places = (
        (block, BLK, mid, mid, 1),
        (low, BLK, pl.ds(0, DEEP), mid, 1),
        (high, BLK, pl.ds(DEEP + BLK, DEEP), mid, 1),
        (mate, DEEP, mid, pl.ds(above_mate * (DEEP + BLK), DEEP), 2 * above_mate),
        (away, DEEP, mid, pl.ds(side_c * (DEEP + BLK), DEEP), 2 * side_c),
    )
    planes, fields = [], []
    for src, count, xs, ys, which in places:
        rows = pl.ds(pl.multiple_of(which * BLK, BLK), BLK)
        planes.append((src.at[:, count], cond.at[xs, rows]))
        planes.append((src.at[:, count + 1], faces.at[xs, which]))
        fields.append((src.at[:, pl.ds(0, count)], fa.at[xs, ys]))
    fields.append((block.at[:, pl.ds(0, BLK)], own))
    copies = [
        pltpu.make_async_copy(src, dst, in_sems.at[n])
        for n, (src, dst) in enumerate(planes + fields)
    ]
    for copy in copies:
        copy.start()

    def clear(i, carry):
        for j in range(DEEP):
            fa[i, j] = zero
            fa[i, EXT - 1 - j] = zero
            fa[EXT - 1 - i, j] = zero
            fa[EXT - 1 - i, EXT - 1 - j] = zero
        return carry

    lax.fori_loop(0, DEEP, clear, 0)
    for which in (0, 2):
        for i in (0, EXT - 1):
            faces[i, which] = zero
            cond[i, which * BLK : (which + 1) * BLK] = zero

    def put_corners(cbelow, cabove):
        at = 0
        for which_x, i, k in corner_blocks():
            x = i if which_x == 0 else DEEP + BLK + i
            for j in range(DEEP - k):
                fa[x, k + j] = cbelow[at]
                fa[x, DEEP + BLK + j] = cabove[at]
                at += 1
            for src, which in ((cbelow, 0), (cabove, 2)):
                cond[x, which * BLK : (which + 1) * BLK] = src[at]
                faces[x, which] = src[at + 1]
            at += 2

    @pl.when(side_c == 0)
    def _():
        put_corners(caway, cmate)

    @pl.when(side_c == 1)
    def _():
        put_corners(cmate, caway)

    for copy in copies[: len(planes)]:
        copy.wait()

    marked[...] = jnp.zeros_like(marked)

    def mark_rows(x, carry):
        for which in range(3):
            marked[which, pl.ds(x, 1)] = faces[x, which, 0:1]
        return carry

    lax.fori_loop(0, EXT, mark_rows, 0)
    marks_copy = pltpu.make_async_copy(marked, marked_s, sem)
    marks_copy.start()

    wide_lane = lax.broadcasted_iota(jnp.int32, (ROWS, NZ), 1)

    def conductances(x, carry):
        here = cond[x]
        cx[x] = harmonic(here, cond[jnp.minimum(x + 1, EXT - 1)])
        cy[x] = harmonic(here, pltpu.roll(here, ROWS - 1, 0))
        cz[x] = jnp.where(
            wide_lane == NZ - 1, 0.0, harmonic(here, pltpu.roll(here, NZ - 1, 1))
        )
        return carry

    lax.fori_loop(0, EXT, conductances, 0)

    def diagonals(x, carry):
        face = jnp.concatenate([faces[x, 0], faces[x, 1], faces[x, 2]], axis=0)
        contact = jnp.where(
            wide_lane == 0,
            pltpu.roll(face, NZ - CONTACT, 1),
            jnp.where(
                wide_lane == NZ - 1, pltpu.roll(face, NZ - 2 - CONTACT, 1), 0.0
            ),
        )
        own_y = cy[x]
        own_z = cz[x]
        total = (
            contact
            + cx[x]
            + cx[jnp.maximum(x - 1, 0)]
            + own_y
            + pltpu.roll(own_y, 1, 0)
            + own_z
            + pltpu.roll(own_z, 1, 1)
        )
        positive = total > 0
        diag[x] = total
        safe = jnp.where(positive, total, 1.0)
        root = lax.rsqrt(safe)
        root = root * (1.5 - 0.5 * safe * root * root)
        scale[x] = jnp.where(positive, root, 0.0)
        return carry

    lax.fori_loop(0, EXT, diagonals, 0)

    def at_row(ref, x, y):
        return ref[x, pl.ds(y + YOFF, 1), :]

    def along_z(src, x, y):
        weight, here = at_row(cz, x, y), src[x, y]
        return weight * pltpu.roll(here, NZ - 1, 1) + pltpu.roll(weight * here, 1, 1)

    def sweep(radius, src, finish):
        lo, hi = DEEP - radius, DEEP + BLK + radius
        for y in range(lo, hi):
            za[y] = along_z(src, lo, y)

        def row(x, ready, coming):
            below, here = src[x, lo - 1], src[x, lo]
            for y in range(lo, hi):
                coming[y] = along_z(src, x + 1, y)
                above = src[x, y + 1]
                total = (
                    at_row(cx, x - 1, y) * src[x - 1, y]
                    + at_row(cx, x, y) * src[x + 1, y]
                    + at_row(cy, x, y - 1) * below
                    + at_row(cy, x, y) * above
                    + ready[y]
                )
                finish(x, y, here, total)
                below, here = here, above

        def two_rows(i, carry):
            row(lo + 2 * i, za, zb)
            row(lo + 2 * i + 1, zb, za)
            return carry

        lax.fori_loop(0, (hi - lo) // 2, two_rows, 0)

    def residual(x, y, here, total):
        fb[x, y] = at_row(scale, x, y) * (total - at_row(diag, x, y) * here)

    for copy in copies[len(planes) :]:
        copy.wait()
    sweep(DEEP - 1, fa, residual)
    marks_copy.wait()

    def add_sources(x, carry):
        for which in range(3):

            @pl.when(marked_s[which, x, MARK] > 0)
            def _():
                face = faces[x, which]
                start = (1, DEEP, DEEP + BLK)[which]
                stop = (DEEP, DEEP + BLK, EXT - 1)[which]
                for y in range(start, stop):
                    spot = (y + YOFF, y - DEEP, y - DEEP - BLK)[which]
                    source = jnp.where(
                        first_lane,
                        pltpu.roll(face, (NZ - spot) % NZ, 1),
                        jnp.where(
                            last_lane, pltpu.roll(face, NZ - 1 - UPPER - spot, 1), 0.0
                        ),
                    )
                    fb[x, y] = fb[x, y] + at_row(scale, x, y) * source

        return carry

    lax.fori_loop(1, EXT - 1, add_sources, 0)

    def rescale(x, carry):
        here = scale[x]
        cx[x] = cx[x] * here * scale[jnp.minimum(x + 1, EXT - 1)]
        cy[x] = cy[x] * here * pltpu.roll(here, ROWS - 1, 0)
        cz[x] = cz[x] * here * pltpu.roll(here, NZ - 1, 1)
        return carry

    lax.fori_loop(0, EXT, rescale, 0)

    def mixed(dst, base, factor):
        def finish(x, y, here, total):
            dst[x, y] = factor * base[x, y] + total

        return finish

    def mapped(dst):
        def finish(x, y, here, total):
            dst[x, y] = here - total

        return finish

    def smooth(radius, base, one, two):
        sweep(radius + 2, base, mixed(one, base, MIX[0]))
        sweep(radius + 1, one, mixed(two, base, MIX[1]))
        sweep(radius, two, mixed(one, base, MIX[2]))

    smooth(5, fb, fa, fc)
    sweep(4, fa, mapped(fc))
    gram_first = gram(fa, (fb, fc), DEEP)

    def save(x, carry):
        for y in range(BLK):
            ub[x, y] = fa[DEEP + x, DEEP + y]
        return carry

    lax.fori_loop(0, BLK, save, 0)
    copy_u = pltpu.make_async_copy(ub, out_u, out_sems.at[0])
    copy_u.start()
    smooth(1, fc, fb, fa)
    copy_z = pltpu.make_async_copy(fb.at[mid, mid], out_z, out_sems.at[1])
    copy_z.start()
    sweep(0, fb, mapped(fa))
    gram_second = gram(fb, (fc, fa), DEEP)

    def save_scale(x, carry):
        out_scale[x] = scale[DEEP + x, BLK : 2 * BLK]
        return carry

    lax.fori_loop(0, BLK, save_scale, 0)

    volt[...] = jnp.zeros_like(volt)
    elane = lax.broadcasted_iota(jnp.int32, (PATS, ELECTRODES), 1)
    half = BLK // PATCH

    def electrode(i, carry):
        mark = marks[i]

        @pl.when(mark > 0)
        def _():
            face = i // (half * half)
            x0 = (i // half) % half * PATCH
            y0 = i % half * PATCH
            wanted = lane == face * (NZ - 1)
            sums = [zero, zero, zero]
            for dx in range(PATCH):
                for dy in range(PATCH):
                    x, y = x0 + dx, y0 + dy
                    weight = out_scale[x, pl.ds(y, 1), :]
                    sums[0] += own[x, y]
                    sums[1] += weight * ub[x, y]
                    sums[2] += weight * fb[DEEP + x, DEEP + y]
            for f in range(3):
                total = jnp.sum(jnp.where(wanted, sums[f], 0.0), axis=1, keepdims=True)
                volt[f] = volt[f] + jnp.where(elane == mark - 1, total, 0.0)

        return carry

    lax.fori_loop(0, 2 * half * half, electrode, 0)

    per = ELECTRODES // 8
    empty = jnp.zeros((PATS, 3 * per), F32)
    grams = jnp.concatenate([empty, gram_first], axis=1)
    rest = jnp.concatenate(
        [gram_second[:8], gram_second[8:], jnp.zeros((8, NZ - 4 * PATS), F32)], axis=1
    )
    for d in range(8):
        tile, spot = d * per // NZ, d * per % NZ
        picked = grams
        for f in range(3):
            part = volt[f, :, tile * NZ : (tile + 1) * NZ]
            part = pltpu.roll(part, (per * f - spot) % NZ, 1)
            inside = (lane >= per * f) & (lane < per * (f + 1))
            picked = jnp.where(inside, part, picked)
        out_chunk[d, 0:PATS] = picked
        out_chunk[d, PATS:] = rest
    copy_u.wait()
    copy_z.wait()


def main_call(side, marks, block, low, high, mate, away, cmate, caway):
    shape = jax.ShapeDtypeStruct
    field = pltpu.VMEM((EXT, EXT, PATS, NZ), F32)
    plane = pltpu.VMEM((EXT, ROWS, NZ), F32)
    return pl.pallas_call(
        main_kernel,
        out_shape=(
            shape((BLK, BLK, PATS, NZ), F32),
            shape((BLK, BLK, PATS, NZ), F32),
            shape((BLK, BLK, NZ), F32),
            shape((8, PATS + 8, NZ), F32),
        ),
        in_specs=[SM, SM] + [HB] * 5 + [VM] * 2,
        out_specs=(HB, HB, VM, VM),
        scratch_shapes=[
            pltpu.VMEM((BLK, BLK, PATS, NZ), F32),
            pltpu.VMEM((BLK, BLK, PATS, NZ), F32),
            field, field, field,
            pltpu.VMEM((EXT, PATS, NZ), F32),
            pltpu.VMEM((EXT, PATS, NZ), F32),
            pltpu.VMEM((EXT, 3, PATS, NZ), F32),
            plane, plane, plane, plane, plane, plane,
            pltpu.VMEM((3, PATS, ELECTRODES), F32),
            pltpu.VMEM((3, MARKROWS, NZ), F32),
            pltpu.SMEM((3, MARKROWS, NZ), F32),
            pltpu.SemaphoreType.DMA,
            pltpu.SemaphoreType.DMA((16,)),
            pltpu.SemaphoreType.DMA((2,)),
        ],
        compiler_params=vmem(60),
    )(side, marks, block, low, high, mate, away, cmate, caway)


def solve_kernel(parts, out_mix, out_volt):
    volts = parts[0, 0:PATS]
    rest = parts[0, PATS:]
    for i in range(1, parts.shape[0]):
        volts = volts + parts[i, 0:PATS]
        rest = rest + parts[i, PATS:]
    lane = lax.broadcasted_iota(jnp.int32, (PATS, NZ), 1)
    second = jnp.concatenate([rest, pltpu.roll(rest, NZ - 2 * PATS, 1)], axis=0)

    a_at, b_at = (volts, NZ - 2 * PATS), (volts, NZ - PATS)
    c_at, e_at = (second, 0), (second, PATS)

    def move(source, target):
        return pltpu.roll(source[0], (target - source[1]) % NZ, 1)

    def pick(first, second, third):
        return jnp.where(
            lane < PATS,
            move(first, 0),
            jnp.where(
                lane < 2 * PATS,
                move(second, PATS),
                jnp.where(lane < 3 * PATS, move(third, 2 * PATS), 0.0),
            ),
        )

    table = jnp.concatenate([pick(b_at, c_at, a_at), pick(c_at, e_at, b_at)], axis=0)
    rows = lax.broadcasted_iota(jnp.int32, (2 * PATS, NZ), 0)
    for k in range(2 * PATS):
        pivot = table[k : k + 1] / table[k : k + 1, k : k + 1]
        table = jnp.where(rows == k, pivot, table - table[:, k : k + 1] * pivot)
    mix = table[:, 2 * PATS : 3 * PATS]
    eye = (
        lax.broadcasted_iota(jnp.int32, (PATS, PATS), 0)
        == lax.broadcasted_iota(jnp.int32, (PATS, PATS), 1)
    ).astype(F32)
    turned = lax.dot_general(
        eye, mix, (((1,), (1,)), ((), ())), precision=HIGHEST, preferred_element_type=F32
    )
    out_mix[...] = turned
    per = ELECTRODES // 8
    fields = jnp.concatenate(
        [pltpu.roll(volts, NZ - per, 1), pltpu.roll(volts, NZ - 2 * per, 1)], axis=0
    )
    total = volts + jnp.dot(turned, fields, precision=HIGHEST, preferred_element_type=F32)
    out_volt[...] = total * (1.0 / (PATCH * PATCH))


def solve_small(parts):
    shape = jax.ShapeDtypeStruct
    return pl.pallas_call(
        solve_kernel,
        out_shape=(shape((PATS, 2 * PATS), F32), shape((PATS, NZ), F32)),
        in_specs=[VM],
        out_specs=(VM, VM),
        compiler_params=vmem(16),
    )(parts)


PARTS = 4


def update_kernel(
    mix, scale, start_h, u_h, z_h, out_h, start, u, z, out, in_sems, out_sems
):
    count = BLK // PARTS
    reads, writes = [], []
    for n in range(PARTS):
        xs = pl.ds(n * count, count)
        pairs = ((u_h.at[xs], u.at[xs]), (z_h.at[xs], z.at[xs]), (start_h.at[:, xs], start.at[:, xs]))
        reads.append(
            [
                pltpu.make_async_copy(src, dst, in_sems.at[3 * n + m])
                for m, (src, dst) in enumerate(pairs)
            ]
        )
        writes.append(pltpu.make_async_copy(out.at[:, xs], out_h.at[:, xs], out_sems.at[n]))
        for copy in reads[n]:
            copy.start()
    left = jnp.concatenate(
        [jnp.concatenate([part] * 3, axis=1) for part in split3(mix[...])], axis=0
    )

    def row(x, carry):
        data = jnp.concatenate(
            [
                jnp.concatenate([field[x, y] for y in range(BLK)], axis=1)
                for field in (u, z)
            ],
            axis=0,
        )
        right = jnp.concatenate(split3(data), axis=0)
        both = jnp.dot(left, right, preferred_element_type=F32)
        both = both[:PATS] + (both[PATS : 2 * PATS] + both[2 * PATS :])
        change = jnp.stack(
            [
                both[:, y * NZ : (y + 1) * NZ] * scale[x, pl.ds(y, 1), :]
                for y in range(BLK)
            ],
            axis=0,
        )
        out[:, x] = start[:, x] + pltpu.einshape("ypz->pyz", change)
        return carry

    for n in range(PARTS):
        for copy in reads[n]:
            copy.wait()
        lax.fori_loop(n * count, (n + 1) * count, row, 0)
        writes[n].start()
    for copy in writes:
        copy.wait()


def update(mix, start, u, z, scale):
    block = pltpu.VMEM((BLK, BLK, PATS, NZ), F32)
    return pl.pallas_call(
        update_kernel,
        out_shape=jax.ShapeDtypeStruct(start.shape, F32),
        in_specs=[VM, VM, HB, HB, HB],
        out_specs=HB,
        scratch_shapes=[
            pltpu.VMEM((PATS, BLK, BLK, NZ), F32), block, block,
            pltpu.VMEM((PATS, BLK, BLK, NZ), F32),
            pltpu.SemaphoreType.DMA((3 * PARTS,)),
            pltpu.SemaphoreType.DMA((PARTS,)),
        ],
        compiler_params=vmem(60),
    )(mix, scale, start, u, z)


def face_blocks(electrode_map, currents, contact_gain):
    numbers = jnp.arange(1, ELECTRODES + 1, dtype=jnp.int32)
    onehot = (electrode_map[..., None] == numbers).astype(F32)
    contact = jnp.einsum("fxye,e->xyf", onehot, contact_gain, precision=HIGHEST)
    source = jnp.einsum("fxye,ep->fxpy", onehot, currents, precision=HIGHEST)
    gap = lambda width: jnp.zeros((BLK, PATS, width), F32)
    marked = (jnp.max(electrode_map, axis=(0, 2)) > 0).astype(F32)
    marked = jnp.broadcast_to(marked[:, None, None], (BLK, PATS, 1))
    return jnp.concatenate(
        [
            source[0], gap(CONTACT - BLK), contact, marked, gap(UPPER - MARK - 1),
            source[1], gap(NZ - UPPER - BLK),
        ],
        axis=2,
    )


def body(start_field, currents, electrode_map, contact_gain, region_label, region_cond, texture):
    gx, gy = lax.axis_size(GX), lax.axis_size(GY)
    side = lax.axis_index("c").astype(jnp.int32).reshape(1)
    marks = electrode_map[:, ::PATCH, ::PATCH].reshape(-1)
    face = face_blocks(electrode_map, currents, contact_gain)
    block, up, down, mate, away = pack(
        side, region_cond, start_field, region_label, texture, face
    )
    rise = [(i, i + 1) for i in range(gx - 1)]
    fall = [(j, i) for i, j in rise]
    pairs = [(i, i + 1) for i in range(0, gy, 2)]
    gaps = [(i, i + 1) for i in range(1, gy - 1, 2)]
    within = pairs + [(j, i) for i, j in pairs]
    across = gaps + [(j, i) for i, j in gaps]
    low = lax.ppermute(up, GX, rise)
    high = lax.ppermute(down, GX, fall)
    away = lax.ppermute(away, GY, across)
    mate = lax.ppermute(mate, GY, within)
    cmate, caway = corners(side, low, high)
    caway = lax.ppermute(caway, GY, across)
    cmate = lax.ppermute(cmate, GY, within)
    u, z, scale, chunk = main_call(
        side, marks, block, low, high, mate, away, cmate, caway
    )
    nx, nz = lax.axis_size("x"), lax.axis_size("z")
    parts = jnp.broadcast_to(chunk[None], (nx,) + chunk.shape)
    parts = parts.reshape((nx * gy,) + chunk.shape[1:])
    parts = lax.all_to_all(parts, ("x", "y", "c"), 0, 0, tiled=True)
    chunk = jnp.sum(parts, axis=0)
    parts = jnp.broadcast_to(chunk[None], (nz,) + chunk.shape)
    parts = lax.all_to_all(parts, "z", 0, 0, tiled=True)
    mix, volt = solve_small(parts)
    volts = jnp.broadcast_to(volt[None], (gy,) + volt.shape)
    volts = lax.all_to_all(volts, GY, 0, 0, tiled=True)
    result = update(mix, start_field, u, z, scale)
    per = ELECTRODES // gy
    voltages = volts[:, :, :per].transpose(1, 0, 2).reshape(PATS, ELECTRODES)
    return result, voltages


def solution(mesh):
    torus = Mesh(mesh.devices.reshape(8, 4, 4, 2), GX + GY)
    placed = (
        P(None, GX, GY, None),
        P(),
        P(None, GX, GY),
        P(),
        P(GX, GY, None),
        P(),
        P(GX, GY, None),
    )
    return jax.shard_map(
        body,
        mesh=torus,
        in_specs=placed,
        out_specs=(P(None, GX, GY, None), P()),
        check_vma=False,
    )
```

```python
import functools

import jax
import jax.numpy as jnp
import numpy as np
from jax import lax
from jax.experimental import pallas as pl
from jax.experimental.pallas import tpu as pltpu
from jax.sharding import Mesh, PartitionSpec as P

ELECTRODES = 256
REGIONS = 8
PATCH = 2
SWEEPS = 3
CHEB_LOW = 0.1
CHEB_HIGH = 2.0

GX = ("z", "x")
GY = ("y", "c")
PATS = 16
BLK = 16
NZ = 128
DEEP = 9
EXT = BLK + 2 * DEEP
ROWS = 3 * BLK
YOFF = BLK - DEEP
COND = BLK
FACE = BLK + 1
UPPER = 64
CONTACT = 32
MARKROWS = 40

F32 = jnp.float32
BF16 = jnp.bfloat16
HIGHEST = lax.Precision.HIGHEST


def polynomial():
    middle = 0.5 * (CHEB_HIGH + CHEB_LOW)
    radius = 0.5 * (CHEB_HIGH - CHEB_LOW)
    sharp = middle / radius
    rho = 1.0 / sharp
    step = np.array([1.0])
    n_of_s = np.array([1.0, -1.0])
    update = np.array([1.0 / middle])
    iterate = update
    for _ in range(SWEEPS):
        defect = np.polynomial.polynomial.polysub(
            step, np.polynomial.polynomial.polymul(n_of_s, iterate)
        )
        rho_next = 1.0 / (2.0 * sharp - rho)
        update = np.polynomial.polynomial.polyadd(
            rho_next * rho * update, 2.0 * rho_next / radius * defect
        )
        iterate = np.polynomial.polynomial.polyadd(iterate, update)
        rho = rho_next
    return [float(v) for v in iterate]


E0, E1, E2, E3 = polynomial()
MIX = (E2 / E3, E1 / E3, E0 / E3)


def corner_blocks():
    rows = [(0, i, DEEP - i) for i in range(1, DEEP)]
    rows += [(1, i, i + 1) for i in range(DEEP - 1)]
    return rows


CORNER = sum(DEEP - k for _, _, k in corner_blocks()) + 2 * len(corner_blocks())


def vmem(mib):
    return pltpu.CompilerParams(vmem_limit_bytes=mib * 1024 * 1024)


VM = pl.BlockSpec(memory_space=pltpu.VMEM)
HB = pl.BlockSpec(memory_space=pltpu.HBM)
SM = pl.BlockSpec(memory_space=pltpu.SMEM)


def pack_kernel(
    side, cond, start, label, texture, face, out, up, down, mate, away, block, sem
):
    side_c = side[0]

    def row(x, carry):
        block[x, 0:BLK] = pltpu.einshape("pyz->ypz", start[:, x])
        lab = label[x]
        value = jnp.zeros((BLK, NZ), F32)
        for region in range(REGIONS):
            value = jnp.where(lab == region, cond[region], value)
        block[x, COND] = value * texture[x]
        block[x, FACE] = face[x]
        return carry

    lax.fori_loop(0, BLK, row, 0)
    copy = pltpu.make_async_copy(block, out, sem)
    copy.start()
    base_mate = (BLK - DEEP) * (1 - side_c)
    base_away = (BLK - DEEP) * side_c

    def faces(x, carry):
        for j in range(DEEP):
            mate[x, j] = block[x, base_mate + j]
            away[x, j] = block[x, base_away + j]
        for j in range(2):
            mate[x, DEEP + j] = block[x, COND + j]
            away[x, DEEP + j] = block[x, COND + j]
        return carry

    lax.fori_loop(0, BLK, faces, 0)

    def ends(x, carry):
        for j in range(BLK + 2):
            up[x, j] = block[BLK - DEEP + x, j]
            down[x, j] = block[x, j]
        return carry

    lax.fori_loop(0, DEEP, ends, 0)
    copy.wait()


def pack(side, region_cond, start, label, texture, face):
    shape = jax.ShapeDtypeStruct
    return pl.pallas_call(
        pack_kernel,
        out_shape=(
            shape((BLK, BLK + 2, PATS, NZ), F32),
            shape((DEEP, BLK + 2, PATS, NZ), F32),
            shape((DEEP, BLK + 2, PATS, NZ), F32),
            shape((BLK, DEEP + 2, PATS, NZ), F32),
            shape((BLK, DEEP + 2, PATS, NZ), F32),
        ),
        in_specs=[SM, SM, VM, VM, VM, VM],
        out_specs=(HB,) + (VM,) * 4,
        scratch_shapes=[
            pltpu.VMEM((BLK, BLK + 2, PATS, NZ), F32),
            pltpu.SemaphoreType.DMA,
        ],
        compiler_params=vmem(40),
    )(side, region_cond, start, label, texture, face)


def corner_kernel(side, low, high, mate, away):
    side_c = side[0]
    at = 0
    for which, i, k in corner_blocks():
        src = low if which == 0 else high
        count = DEEP - k
        base_mate = (BLK - count) * (1 - side_c)
        base_away = (BLK - count) * side_c
        for j in range(count):
            mate[at] = src[i, base_mate + j]
            away[at] = src[i, base_away + j]
            at += 1
        for j in range(2):
            mate[at] = src[i, COND + j]
            away[at] = src[i, COND + j]
            at += 1


def corners(side, low, high):
    shape = jax.ShapeDtypeStruct((CORNER, PATS, NZ), F32)
    return pl.pallas_call(
        corner_kernel,
        out_shape=(shape, shape),
        in_specs=[SM, VM, VM],
        out_specs=(VM, VM),
        compiler_params=vmem(24),
    )(side, low, high)


def harmonic(own, other):
    total = own + other
    return 2.0 * own * other / jnp.where(total > 0, total, 1.0)


def split(value):
    high = value.astype(BF16)
    return high, (value - high.astype(F32)).astype(BF16)


def split3(value):
    high = value.astype(BF16)
    rest = value - high.astype(F32)
    middle = rest.astype(BF16)
    return high, middle, (rest - middle.astype(F32)).astype(BF16)


def gram(first, seconds, origin):
    width = 2 * PATS * len(seconds)

    def row(i, total):
        x = origin + i

        def flat(ref):
            return jnp.concatenate([ref[x, origin + j] for j in range(BLK)], axis=1)

        left = jnp.concatenate(split(flat(first)), axis=0)
        parts = [split(flat(ref)) for ref in seconds]
        right = jnp.concatenate([p[0] for p in parts] + [p[1] for p in parts], axis=0)
        return total + lax.dot_general(
            left, right, (((1,), (1,)), ((), ())), preferred_element_type=F32
        )

    total = lax.fori_loop(0, BLK, row, jnp.zeros((2 * PATS, width), F32))
    total = total[:PATS] + total[PATS:]
    half = width // 2
    return total[:, :half] + total[:, half:]


def main_kernel(
    side, marks, block, low, high, mate, away, cmate, caway,
    out_u, out_z, out_scale, out_chunk,
    own, ub, fa, fb, fc, za, zb, faces, cond, cx, cy, cz, diag, scale, volt,
    marked, marked_s, sem, in_sems, out_sems,
):
    side_c = side[0]
    lane = lax.broadcasted_iota(jnp.int32, (PATS, NZ), 1)
    first_lane = lane == 0
    last_lane = lane == NZ - 1

    zero = jnp.zeros((PATS, NZ), F32)
    mid = pl.ds(DEEP, BLK)
    above_mate = 1 - side_c
    places = (
        (block, BLK, mid, mid, 1),
        (low, BLK, pl.ds(0, DEEP), mid, 1),
        (high, BLK, pl.ds(DEEP + BLK, DEEP), mid, 1),
        (mate, DEEP, mid, pl.ds(above_mate * (DEEP + BLK), DEEP), 2 * above_mate),
        (away, DEEP, mid, pl.ds(side_c * (DEEP + BLK), DEEP), 2 * side_c),
    )
    planes, fields = [], []
    for src, count, xs, ys, which in places:
        rows = pl.ds(pl.multiple_of(which * BLK, BLK), BLK)
        planes.append((src.at[:, count], cond.at[xs, rows]))
        planes.append((src.at[:, count + 1], faces.at[xs, which]))
        fields.append((src.at[:, pl.ds(0, count)], fa.at[xs, ys]))
    fields.append((block.at[:, pl.ds(0, BLK)], own))
    copies = [
        pltpu.make_async_copy(src, dst, in_sems.at[n])
        for n, (src, dst) in enumerate(planes + fields)
    ]
    for copy in copies[:-1]:
        copy.start()

    def clear(i, carry):
        for j in range(DEEP):
            fa[i, j] = zero
            fa[i, EXT - 1 - j] = zero
            fa[EXT - 1 - i, j] = zero
            fa[EXT - 1 - i, EXT - 1 - j] = zero
        return carry

    lax.fori_loop(0, DEEP, clear, 0)
    for which in (0, 2):
        for i in (0, EXT - 1):
            faces[i, which] = zero
            cond[i, which * BLK : (which + 1) * BLK] = zero

    def put_corners(cbelow, cabove):
        at = 0
        for which_x, i, k in corner_blocks():
            x = i if which_x == 0 else DEEP + BLK + i
            for j in range(DEEP - k):
                fa[x, k + j] = cbelow[at]
                fa[x, DEEP + BLK + j] = cabove[at]
                at += 1
            for src, which in ((cbelow, 0), (cabove, 2)):
                cond[x, which * BLK : (which + 1) * BLK] = src[at]
                faces[x, which] = src[at + 1]
            at += 2

    @pl.when(side_c == 0)
    def _():
        put_corners(caway, cmate)

    @pl.when(side_c == 1)
    def _():
        put_corners(cmate, caway)

    for copy in copies[: len(planes)]:
        copy.wait()

    marked[...] = jnp.zeros_like(marked)

    def mark_rows(x, carry):
        for which in range(3):
            marked[which, pl.ds(x, 1)] = jnp.sum(faces[x, which], axis=0, keepdims=True)
        return carry

    lax.fori_loop(0, EXT, mark_rows, 0)
    marks_copy = pltpu.make_async_copy(marked, marked_s, sem)
    marks_copy.start()

    wide_lane = lax.broadcasted_iota(jnp.int32, (ROWS, NZ), 1)

    def conductances(x, carry):
        here = cond[x]
        cx[x] = harmonic(here, cond[jnp.minimum(x + 1, EXT - 1)])
        cy[x] = harmonic(here, pltpu.roll(here, ROWS - 1, 0))
        cz[x] = jnp.where(
            wide_lane == NZ - 1, 0.0, harmonic(here, pltpu.roll(here, NZ - 1, 1))
        )
        return carry

    lax.fori_loop(0, EXT, conductances, 0)

    def diagonals(x, carry):
        face = jnp.concatenate([faces[x, 0], faces[x, 1], faces[x, 2]], axis=0)
        contact = jnp.where(
            wide_lane == 0,
            pltpu.roll(face, NZ - CONTACT, 1),
            jnp.where(
                wide_lane == NZ - 1, pltpu.roll(face, NZ - 2 - CONTACT, 1), 0.0
            ),
        )
        own_y = cy[x]
        own_z = cz[x]
        total = (
            contact
            + cx[x]
            + cx[jnp.maximum(x - 1, 0)]
            + own_y
            + pltpu.roll(own_y, 1, 0)
            + own_z
            + pltpu.roll(own_z, 1, 1)
        )
        positive = total > 0
        diag[x] = total
        safe = jnp.where(positive, total, 1.0)
        root = lax.rsqrt(safe)
        root = root * (1.5 - 0.5 * safe * root * root)
        scale[x] = jnp.where(positive, root, 0.0)
        return carry

    lax.fori_loop(0, EXT, diagonals, 0)

    def at_row(ref, x, y):
        return ref[x, pl.ds(y + YOFF, 1), :]

    def along_z(src, x, y):
        weight, here = at_row(cz, x, y), src[x, y]
        return weight * pltpu.roll(here, NZ - 1, 1) + pltpu.roll(weight * here, 1, 1)

    def sweep(radius, src, finish):
        lo, hi = DEEP - radius, DEEP + BLK + radius
        for y in range(lo, hi):
            za[y] = along_z(src, lo, y)

        def row(x, ready, coming):
            below, here = src[x, lo - 1], src[x, lo]
            for y in range(lo, hi):
                coming[y] = along_z(src, x + 1, y)
                above = src[x, y + 1]
                total = (
                    at_row(cx, x - 1, y) * src[x - 1, y]
                    + at_row(cx, x, y) * src[x + 1, y]
                    + at_row(cy, x, y - 1) * below
                    + at_row(cy, x, y) * above
                    + ready[y]
                )
                finish(x, y, here, total)
                below, here = here, above

        def two_rows(i, carry):
            row(lo + 2 * i, za, zb)
            row(lo + 2 * i + 1, zb, za)
            return carry

        lax.fori_loop(0, (hi - lo) // 2, two_rows, 0)

    def residual(x, y, here, total):
        fb[x, y] = at_row(scale, x, y) * (total - at_row(diag, x, y) * here)

    for copy in copies[len(planes) : -1]:
        copy.wait()
    copies[-1].start()
    sweep(DEEP - 1, fa, residual)
    marks_copy.wait()
    copies[-1].wait()

    def add_sources(x, carry):
        for which in range(3):

            @pl.when(marked_s[which, x, CONTACT] + marked_s[which, x, CONTACT + 1] > 0)
            def _():
                face = faces[x, which]
                start = (1, DEEP, DEEP + BLK)[which]
                stop = (DEEP, DEEP + BLK, EXT - 1)[which]
                for y in range(start, stop):
                    spot = (y + YOFF, y - DEEP, y - DEEP - BLK)[which]
                    source = jnp.where(
                        first_lane,
                        pltpu.roll(face, (NZ - spot) % NZ, 1),
                        jnp.where(
                            last_lane, pltpu.roll(face, NZ - 1 - UPPER - spot, 1), 0.0
                        ),
                    )
                    fb[x, y] = fb[x, y] + at_row(scale, x, y) * source

        return carry

    lax.fori_loop(1, EXT - 1, add_sources, 0)

    def rescale(x, carry):
        here = scale[x]
        cx[x] = cx[x] * here * scale[jnp.minimum(x + 1, EXT - 1)]
        cy[x] = cy[x] * here * pltpu.roll(here, ROWS - 1, 0)
        cz[x] = cz[x] * here * pltpu.roll(here, NZ - 1, 1)
        return carry

    lax.fori_loop(0, EXT, rescale, 0)

    def mixed(dst, base, factor):
        def finish(x, y, here, total):
            dst[x, y] = factor * base[x, y] + total

        return finish

    def mapped(dst):
        def finish(x, y, here, total):
            dst[x, y] = here - total

        return finish

    def smooth(radius, base, one, two):
        sweep(radius + 2, base, mixed(one, base, MIX[0]))
        sweep(radius + 1, one, mixed(two, base, MIX[1]))
        sweep(radius, two, mixed(one, base, MIX[2]))

    smooth(5, fb, fa, fc)
    sweep(4, fa, mapped(fc))
    gram_first = gram(fa, (fb, fc), DEEP)

    def save(x, carry):
        for y in range(BLK):
            ub[x, y] = fa[DEEP + x, DEEP + y]
        return carry

    lax.fori_loop(0, BLK, save, 0)
    copy_u = pltpu.make_async_copy(ub, out_u, out_sems.at[0])
    copy_u.start()
    smooth(1, fc, fb, fa)
    copy_z = pltpu.make_async_copy(fb.at[mid, mid], out_z, out_sems.at[1])
    copy_z.start()
    sweep(0, fb, mapped(fa))
    gram_second = gram(fb, (fc, fa), DEEP)

    def save_scale(x, carry):
        out_scale[x] = scale[DEEP + x, BLK : 2 * BLK]
        return carry

    lax.fori_loop(0, BLK, save_scale, 0)

    volt[...] = jnp.zeros_like(volt)
    elane = lax.broadcasted_iota(jnp.int32, (PATS, ELECTRODES), 1)
    half = BLK // PATCH

    def electrode(i, carry):
        mark = marks[i]

        @pl.when(mark > 0)
        def _():
            face = i // (half * half)
            x0 = (i // half) % half * PATCH
            y0 = i % half * PATCH
            wanted = lane == face * (NZ - 1)
            sums = [zero, zero, zero]
            for dx in range(PATCH):
                for dy in range(PATCH):
                    x, y = x0 + dx, y0 + dy
                    weight = out_scale[x, pl.ds(y, 1), :]
                    sums[0] += own[x, y]
                    sums[1] += weight * ub[x, y]
                    sums[2] += weight * fb[DEEP + x, DEEP + y]
            for f in range(3):
                total = jnp.sum(jnp.where(wanted, sums[f], 0.0), axis=1, keepdims=True)
                volt[f] = volt[f] + jnp.where(elane == mark - 1, total, 0.0)

        return carry

    lax.fori_loop(0, 2 * half * half, electrode, 0)

    per = ELECTRODES // 8
    empty = jnp.zeros((PATS, 3 * per), F32)
    grams = jnp.concatenate([empty, gram_first], axis=1)
    rest = jnp.concatenate(
        [gram_second[:8], gram_second[8:], jnp.zeros((8, NZ - 4 * PATS), F32)], axis=1
    )
    for d in range(8):
        tile, spot = d * per // NZ, d * per % NZ
        picked = grams
        for f in range(3):
            part = volt[f, :, tile * NZ : (tile + 1) * NZ]
            part = pltpu.roll(part, (per * f - spot) % NZ, 1)
            inside = (lane >= per * f) & (lane < per * (f + 1))
            picked = jnp.where(inside, part, picked)
        for copy in range(out_chunk.shape[0]):
            out_chunk[copy, d, 0:PATS] = picked
            out_chunk[copy, d, PATS:] = rest
    copy_u.wait()
    copy_z.wait()


def main_call(side, marks, block, low, high, mate, away, cmate, caway):
    shape = jax.ShapeDtypeStruct
    field = pltpu.VMEM((EXT, EXT, PATS, NZ), F32)
    plane = pltpu.VMEM((EXT, ROWS, NZ), F32)
    return pl.pallas_call(
        main_kernel,
        out_shape=(
            shape((BLK, BLK, PATS, NZ), F32),
            shape((BLK, BLK, PATS, NZ), F32),
            shape((BLK, BLK, NZ), F32),
            shape((4, 8, PATS + 8, NZ), F32),
        ),
        in_specs=[SM, SM] + [HB] * 5 + [VM] * 2,
        out_specs=(HB, HB, VM, VM),
        scratch_shapes=[
            pltpu.VMEM((BLK, BLK, PATS, NZ), F32),
            pltpu.VMEM((BLK, BLK, PATS, NZ), F32),
            field, field, field,
            pltpu.VMEM((EXT, PATS, NZ), F32),
            pltpu.VMEM((EXT, PATS, NZ), F32),
            pltpu.VMEM((EXT, 3, PATS, NZ), F32),
            plane, plane, plane, plane, plane, plane,
            pltpu.VMEM((3, PATS, ELECTRODES), F32),
            pltpu.VMEM((3, MARKROWS, NZ), F32),
            pltpu.SMEM((3, MARKROWS, NZ), F32),
            pltpu.SemaphoreType.DMA,
            pltpu.SemaphoreType.DMA((16,)),
            pltpu.SemaphoreType.DMA((2,)),
        ],
        compiler_params=vmem(60),
    )(side, marks, block, low, high, mate, away, cmate, caway)


def solve_kernel(parts, out_mix, out_volt):
    volts = parts[0, 0:PATS]
    rest = parts[0, PATS:]
    for i in range(1, parts.shape[0]):
        volts = volts + parts[i, 0:PATS]
        rest = rest + parts[i, PATS:]
    lane = lax.broadcasted_iota(jnp.int32, (PATS, NZ), 1)
    second = jnp.concatenate([rest, pltpu.roll(rest, NZ - 2 * PATS, 1)], axis=0)

    a_at, b_at = (volts, NZ - 2 * PATS), (volts, NZ - PATS)
    c_at, e_at = (second, 0), (second, PATS)

    def move(source, target):
        return pltpu.roll(source[0], (target - source[1]) % NZ, 1)

    def pick(first, second, third):
        return jnp.where(
            lane < PATS,
            move(first, 0),
            jnp.where(
                lane < 2 * PATS,
                move(second, PATS),
                jnp.where(lane < 3 * PATS, move(third, 2 * PATS), 0.0),
            ),
        )

    table = jnp.concatenate([pick(b_at, c_at, a_at), pick(c_at, e_at, b_at)], axis=0)
    rows = lax.broadcasted_iota(jnp.int32, (2 * PATS, NZ), 0)
    for k in range(2 * PATS):
        pivot = table[k : k + 1] / table[k : k + 1, k : k + 1]
        table = jnp.where(rows == k, pivot, table - table[:, k : k + 1] * pivot)
    mix = table[:, 2 * PATS : 3 * PATS]
    eye = (
        lax.broadcasted_iota(jnp.int32, (PATS, PATS), 0)
        == lax.broadcasted_iota(jnp.int32, (PATS, PATS), 1)
    ).astype(F32)
    turned = lax.dot_general(
        eye, mix, (((1,), (1,)), ((), ())), precision=HIGHEST, preferred_element_type=F32
    )
    out_mix[...] = turned
    per = ELECTRODES // 8
    fields = jnp.concatenate(
        [pltpu.roll(volts, NZ - per, 1), pltpu.roll(volts, NZ - 2 * per, 1)], axis=0
    )
    total = volts + jnp.dot(turned, fields, precision=HIGHEST, preferred_element_type=F32)
    out_volt[...] = total * (1.0 / (PATCH * PATCH))


def solve_small(parts):
    shape = jax.ShapeDtypeStruct
    return pl.pallas_call(
        solve_kernel,
        out_shape=(shape((PATS, 2 * PATS), F32), shape((PATS, NZ), F32)),
        in_specs=[VM],
        out_specs=(VM, VM),
        compiler_params=vmem(16),
    )(parts)


PARTS = 4


def update_kernel(
    mix, scale, start_h, u_h, z_h, out_h, start, u, z, out, in_sems, out_sems
):
    count = BLK // PARTS
    reads, writes = [], []
    for n in range(PARTS):
        xs = pl.ds(n * count, count)
        pairs = ((u_h.at[xs], u.at[xs]), (z_h.at[xs], z.at[xs]), (start_h.at[:, xs], start.at[:, xs]))
        reads.append(
            [
                pltpu.make_async_copy(src, dst, in_sems.at[3 * n + m])
                for m, (src, dst) in enumerate(pairs)
            ]
        )
        writes.append(pltpu.make_async_copy(out.at[:, xs], out_h.at[:, xs], out_sems.at[n]))
        for copy in reads[n]:
            copy.start()
    left = jnp.concatenate(
        [jnp.concatenate([part] * 3, axis=1) for part in split3(mix[...])], axis=0
    )

    def row(x, carry):
        data = jnp.concatenate(
            [
                jnp.concatenate([field[x, y] for y in range(BLK)], axis=1)
                for field in (u, z)
            ],
            axis=0,
        )
        right = jnp.concatenate(split3(data), axis=0)
        both = jnp.dot(left, right, preferred_element_type=F32)
        both = both[:PATS] + (both[PATS : 2 * PATS] + both[2 * PATS :])
        change = jnp.stack(
            [
                both[:, y * NZ : (y + 1) * NZ] * scale[x, pl.ds(y, 1), :]
                for y in range(BLK)
            ],
            axis=0,
        )
        out[:, x] = start[:, x] + pltpu.einshape("ypz->pyz", change)
        return carry

    for n in range(PARTS):
        for copy in reads[n]:
            copy.wait()
        lax.fori_loop(n * count, (n + 1) * count, row, 0)
        writes[n].start()
    for copy in writes:
        copy.wait()


def update(mix, start, u, z, scale):
    block = pltpu.VMEM((BLK, BLK, PATS, NZ), F32)
    return pl.pallas_call(
        update_kernel,
        out_shape=jax.ShapeDtypeStruct(start.shape, F32),
        in_specs=[VM, VM, HB, HB, HB],
        out_specs=HB,
        scratch_shapes=[
            pltpu.VMEM((PATS, BLK, BLK, NZ), F32), block, block,
            pltpu.VMEM((PATS, BLK, BLK, NZ), F32),
            pltpu.SemaphoreType.DMA((3 * PARTS,)),
            pltpu.SemaphoreType.DMA((PARTS,)),
        ],
        compiler_params=vmem(60),
    )(mix, scale, start, u, z)


def face_blocks(electrode_map, currents, contact_gain):
    numbers = jnp.arange(1, ELECTRODES + 1, dtype=jnp.int32)
    onehot = (electrode_map[..., None] == numbers).astype(F32)
    contact = jnp.einsum("fxye,e->xyf", onehot, contact_gain, precision=HIGHEST)
    source = jnp.einsum("fxye,ep->fxpy", onehot, currents, precision=HIGHEST)
    gap = lambda width: jnp.zeros((BLK, PATS, width), F32)
    return jnp.concatenate(
        [
            source[0], gap(CONTACT - BLK), contact, gap(UPPER - CONTACT - 2),
            source[1], gap(NZ - UPPER - BLK),
        ],
        axis=2,
    )


def body(start_field, currents, electrode_map, contact_gain, region_label, region_cond, texture):
    gx, gy = lax.axis_size(GX), lax.axis_size(GY)
    side = lax.axis_index("c").astype(jnp.int32).reshape(1)
    marks = electrode_map[:, ::PATCH, ::PATCH].reshape(-1)
    face = face_blocks(electrode_map, currents, contact_gain)
    block, up, down, mate, away = pack(
        side, region_cond, start_field, region_label, texture, face
    )
    rise = [(i, i + 1) for i in range(gx - 1)]
    fall = [(j, i) for i, j in rise]
    pairs = [(i, i + 1) for i in range(0, gy, 2)]
    gaps = [(i, i + 1) for i in range(1, gy - 1, 2)]
    within = pairs + [(j, i) for i, j in pairs]
    across = gaps + [(j, i) for i, j in gaps]
    low = lax.ppermute(up, GX, rise)
    high = lax.ppermute(down, GX, fall)
    away = lax.ppermute(away, GY, across)
    mate = lax.ppermute(mate, GY, within)
    cmate, caway = corners(side, low, high)
    caway = lax.ppermute(caway, GY, across)
    cmate = lax.ppermute(cmate, GY, within)
    u, z, scale, chunk = main_call(
        side, marks, block, low, high, mate, away, cmate, caway
    )
    nz = lax.axis_size("z")
    parts = chunk.reshape((-1,) + chunk.shape[2:])
    parts = lax.all_to_all(parts, ("x", "y", "c"), 0, 0, tiled=True)
    chunk = jnp.sum(parts, axis=0)
    parts = jnp.broadcast_to(chunk[None], (nz,) + chunk.shape)
    parts = lax.all_to_all(parts, "z", 0, 0, tiled=True)
    mix, volt = solve_small(parts)
    volts = jnp.broadcast_to(volt[None], (gy,) + volt.shape)
    volts = lax.all_to_all(volts, GY, 0, 0, tiled=True)
    result = update(mix, start_field, u, z, scale)
    per = ELECTRODES // gy
    voltages = volts[:, :, :per].transpose(1, 0, 2).reshape(PATS, ELECTRODES)
    return result, voltages


def solution(mesh):
    torus = Mesh(mesh.devices.reshape(8, 4, 4, 2), GX + GY)
    placed = (
        P(None, GX, GY, None),
        P(),
        P(None, GX, GY),
        P(),
        P(GX, GY, None),
        P(),
        P(GX, GY, None),
    )
    return jax.shard_map(
        body,
        mesh=torus,
        in_specs=placed,
        out_specs=(P(None, GX, GY, None), P()),
        check_vma=False,
    )
```

```python
import functools

import jax
import jax.numpy as jnp
import numpy as np
from jax import lax
from jax.experimental import pallas as pl
from jax.experimental.pallas import tpu as pltpu
from jax.sharding import Mesh, PartitionSpec as P

ELECTRODES = 256
REGIONS = 8
PATCH = 2
SWEEPS = 3
CHEB_LOW = 0.1
CHEB_HIGH = 2.0

GX = ("z", "x")
GY = ("y", "c")
PATS = 16
BLK = 16
NZ = 128
DEEP = 9
EXT = BLK + 2 * DEEP
ROWS = 3 * BLK
YOFF = BLK - DEEP
COND = BLK
FACE = BLK + 1
UPPER = 64
CONTACT = 32
MARKROWS = 40

F32 = jnp.float32
BF16 = jnp.bfloat16
HIGHEST = lax.Precision.HIGHEST


def polynomial():
    middle = 0.5 * (CHEB_HIGH + CHEB_LOW)
    radius = 0.5 * (CHEB_HIGH - CHEB_LOW)
    sharp = middle / radius
    rho = 1.0 / sharp
    step = np.array([1.0])
    n_of_s = np.array([1.0, -1.0])
    update = np.array([1.0 / middle])
    iterate = update
    for _ in range(SWEEPS):
        defect = np.polynomial.polynomial.polysub(
            step, np.polynomial.polynomial.polymul(n_of_s, iterate)
        )
        rho_next = 1.0 / (2.0 * sharp - rho)
        update = np.polynomial.polynomial.polyadd(
            rho_next * rho * update, 2.0 * rho_next / radius * defect
        )
        iterate = np.polynomial.polynomial.polyadd(iterate, update)
        rho = rho_next
    return [float(v) for v in iterate]


E0, E1, E2, E3 = polynomial()
MIX = (E2 / E3, E1 / E3, E0 / E3)


def corner_blocks():
    rows = [(0, i, DEEP - i) for i in range(1, DEEP)]
    rows += [(1, i, i + 1) for i in range(DEEP - 1)]
    return rows


CORNER = sum(DEEP - k for _, _, k in corner_blocks()) + 2 * len(corner_blocks())


def vmem(mib):
    return pltpu.CompilerParams(vmem_limit_bytes=mib * 1024 * 1024)


VM = pl.BlockSpec(memory_space=pltpu.VMEM)
HB = pl.BlockSpec(memory_space=pltpu.HBM)
SM = pl.BlockSpec(memory_space=pltpu.SMEM)


def pack_kernel(
    side, cond, start, label, texture, face, out, up, down, mate, away, block, sem
):
    side_c = side[0]

    def row(x, carry):
        block[x, 0:BLK] = pltpu.einshape("pyz->ypz", start[:, x])
        lab = label[x]
        value = jnp.zeros((BLK, NZ), F32)
        for region in range(REGIONS):
            value = jnp.where(lab == region, cond[region], value)
        block[x, COND] = value * texture[x]
        block[x, FACE] = face[x]
        return carry

    lax.fori_loop(0, BLK, row, 0)
    copy = pltpu.make_async_copy(block, out, sem)
    copy.start()
    base_mate = (BLK - DEEP) * (1 - side_c)
    base_away = (BLK - DEEP) * side_c

    def faces(x, carry):
        for j in range(DEEP):
            mate[x, j] = block[x, base_mate + j]
            away[x, j] = block[x, base_away + j]
        for j in range(2):
            mate[x, DEEP + j] = block[x, COND + j]
            away[x, DEEP + j] = block[x, COND + j]
        return carry

    lax.fori_loop(0, BLK, faces, 0)

    def ends(x, carry):
        for j in range(BLK + 2):
            up[x, j] = block[BLK - DEEP + x, j]
            down[x, j] = block[x, j]
        return carry

    lax.fori_loop(0, DEEP, ends, 0)
    copy.wait()


def pack(side, region_cond, start, label, texture, face):
    shape = jax.ShapeDtypeStruct
    return pl.pallas_call(
        pack_kernel,
        out_shape=(
            shape((BLK, BLK + 2, PATS, NZ), F32),
            shape((DEEP, BLK + 2, PATS, NZ), F32),
            shape((DEEP, BLK + 2, PATS, NZ), F32),
            shape((BLK, DEEP + 2, PATS, NZ), F32),
            shape((BLK, DEEP + 2, PATS, NZ), F32),
        ),
        in_specs=[SM, SM, VM, VM, VM, VM],
        out_specs=(HB,) + (VM,) * 4,
        scratch_shapes=[
            pltpu.VMEM((BLK, BLK + 2, PATS, NZ), F32),
            pltpu.SemaphoreType.DMA,
        ],
        compiler_params=vmem(57),
    )(side, region_cond, start, label, texture, face)


def corner_kernel(side, low, high, mate, away):
    side_c = side[0]
    at = 0
    for which, i, k in corner_blocks():
        src = low if which == 0 else high
        count = DEEP - k
        base_mate = (BLK - count) * (1 - side_c)
        base_away = (BLK - count) * side_c
        for j in range(count):
            mate[at] = src[i, base_mate + j]
            away[at] = src[i, base_away + j]
            at += 1
        for j in range(2):
            mate[at] = src[i, COND + j]
            away[at] = src[i, COND + j]
            at += 1


def corners(side, low, high):
    shape = jax.ShapeDtypeStruct((CORNER, PATS, NZ), F32)
    return pl.pallas_call(
        corner_kernel,
        out_shape=(shape, shape),
        in_specs=[SM, VM, VM],
        out_specs=(VM, VM),
        compiler_params=vmem(24),
    )(side, low, high)


def harmonic(own, other):
    total = own + other
    return 2.0 * own * other / jnp.where(total > 0, total, 1.0)


def split(value):
    high = value.astype(BF16)
    return high, (value - high.astype(F32)).astype(BF16)


def split3(value):
    high = value.astype(BF16)
    rest = value - high.astype(F32)
    middle = rest.astype(BF16)
    return high, middle, (rest - middle.astype(F32)).astype(BF16)


def gram(first, seconds, origin):
    width = 2 * PATS * len(seconds)

    def row(i, total):
        x = origin + i

        def flat(ref):
            return jnp.concatenate([ref[x, origin + j] for j in range(BLK)], axis=1)

        left = jnp.concatenate(split(flat(first)), axis=0)
        parts = [split(flat(ref)) for ref in seconds]
        right = jnp.concatenate([p[0] for p in parts] + [p[1] for p in parts], axis=0)
        return total + lax.dot_general(
            left, right, (((1,), (1,)), ((), ())), preferred_element_type=F32
        )

    total = lax.fori_loop(0, BLK, row, jnp.zeros((2 * PATS, width), F32))
    total = total[:PATS] + total[PATS:]
    half = width // 2
    return total[:, :half] + total[:, half:]


def main_kernel(
    side, marks, block, low, high, mate, away, cmate, caway,
    out_u, out_z, out_scale, out_chunk,
    own, ub, fa, fb, fc, za, zb, faces, cond, cx, cy, cz, diag, scale, volt,
    marked, marked_s, sem, in_sems, out_sems,
):
    side_c = side[0]
    lane = lax.broadcasted_iota(jnp.int32, (PATS, NZ), 1)
    first_lane = lane == 0
    last_lane = lane == NZ - 1

    zero = jnp.zeros((PATS, NZ), F32)
    mid = pl.ds(DEEP, BLK)
    above_mate = 1 - side_c
    places = (
        (block, BLK, mid, mid, 1),
        (low, BLK, pl.ds(0, DEEP), mid, 1),
        (high, BLK, pl.ds(DEEP + BLK, DEEP), mid, 1),
        (mate, DEEP, mid, pl.ds(above_mate * (DEEP + BLK), DEEP), 2 * above_mate),
        (away, DEEP, mid, pl.ds(side_c * (DEEP + BLK), DEEP), 2 * side_c),
    )
    planes, fields = [], []
    for src, count, xs, ys, which in places:
        rows = pl.ds(pl.multiple_of(which * BLK, BLK), BLK)
        planes.append((src.at[:, count], cond.at[xs, rows]))
        planes.append((src.at[:, count + 1], faces.at[xs, which]))
        fields.append((src.at[:, pl.ds(0, count)], fa.at[xs, ys]))
    fields.append((block.at[:, pl.ds(0, BLK)], own))
    copies = [
        pltpu.make_async_copy(src, dst, in_sems.at[n])
        for n, (src, dst) in enumerate(planes + fields)
    ]
    for copy in copies[:-1]:
        copy.start()

    def clear(i, carry):
        for j in range(DEEP):
            fa[i, j] = zero
            fa[i, EXT - 1 - j] = zero
            fa[EXT - 1 - i, j] = zero
            fa[EXT - 1 - i, EXT - 1 - j] = zero
        return carry

    lax.fori_loop(0, DEEP, clear, 0)
    for which in (0, 2):
        for i in (0, EXT - 1):
            faces[i, which] = zero
            cond[i, which * BLK : (which + 1) * BLK] = zero

    def put_corners(cbelow, cabove):
        at = 0
        for which_x, i, k in corner_blocks():
            x = i if which_x == 0 else DEEP + BLK + i
            for j in range(DEEP - k):
                fa[x, k + j] = cbelow[at]
                fa[x, DEEP + BLK + j] = cabove[at]
                at += 1
            for src, which in ((cbelow, 0), (cabove, 2)):
                cond[x, which * BLK : (which + 1) * BLK] = src[at]
                faces[x, which] = src[at + 1]
            at += 2

    @pl.when(side_c == 0)
    def _():
        put_corners(caway, cmate)

    @pl.when(side_c == 1)
    def _():
        put_corners(cmate, caway)

    for copy in copies[: len(planes)]:
        copy.wait()

    marked[...] = jnp.zeros_like(marked)

    def mark_rows(x, carry):
        for which in range(3):
            marked[which, pl.ds(x, 1)] = jnp.sum(faces[x, which], axis=0, keepdims=True)
        return carry

    lax.fori_loop(0, EXT, mark_rows, 0)
    marks_copy = pltpu.make_async_copy(marked, marked_s, sem)
    marks_copy.start()

    wide_lane = lax.broadcasted_iota(jnp.int32, (ROWS, NZ), 1)

    def conductances(x, carry):
        here = cond[x]
        cx[x] = harmonic(here, cond[jnp.minimum(x + 1, EXT - 1)])
        cy[x] = harmonic(here, pltpu.roll(here, ROWS - 1, 0))
        cz[x] = jnp.where(
            wide_lane == NZ - 1, 0.0, harmonic(here, pltpu.roll(here, NZ - 1, 1))
        )
        return carry

    lax.fori_loop(0, EXT, conductances, 0)

    def diagonals(x, carry):
        face = jnp.concatenate([faces[x, 0], faces[x, 1], faces[x, 2]], axis=0)
        contact = jnp.where(
            wide_lane == 0,
            pltpu.roll(face, NZ - CONTACT, 1),
            jnp.where(
                wide_lane == NZ - 1, pltpu.roll(face, NZ - 2 - CONTACT, 1), 0.0
            ),
        )
        own_y = cy[x]
        own_z = cz[x]
        total = (
            contact
            + cx[x]
            + cx[jnp.maximum(x - 1, 0)]
            + own_y
            + pltpu.roll(own_y, 1, 0)
            + own_z
            + pltpu.roll(own_z, 1, 1)
        )
        positive = total > 0
        diag[x] = total
        safe = jnp.where(positive, total, 1.0)
        root = lax.rsqrt(safe)
        root = root * (1.5 - 0.5 * safe * root * root)
        scale[x] = jnp.where(positive, root, 0.0)
        return carry

    lax.fori_loop(0, EXT, diagonals, 0)

    def at_row(ref, x, y):
        return ref[x, pl.ds(y + YOFF, 1), :]

    def along_z(src, x, y):
        weight, here = at_row(cz, x, y), src[x, y]
        return weight * pltpu.roll(here, NZ - 1, 1) + pltpu.roll(weight * here, 1, 1)

    def sweep(radius, src, finish):
        lo, hi = DEEP - radius, DEEP + BLK + radius
        for y in range(lo, hi):
            za[y] = along_z(src, lo, y)

        def row(x, ready, coming):
            below, here = src[x, lo - 1], src[x, lo]
            for y in range(lo, hi):
                coming[y] = along_z(src, x + 1, y)
                above = src[x, y + 1]
                total = (
                    at_row(cx, x - 1, y) * src[x - 1, y]
                    + at_row(cx, x, y) * src[x + 1, y]
                    + at_row(cy, x, y - 1) * below
                    + at_row(cy, x, y) * above
                    + ready[y]
                )
                finish(x, y, here, total)
                below, here = here, above

        def two_rows(i, carry):
            row(lo + 2 * i, za, zb)
            row(lo + 2 * i + 1, zb, za)
            return carry

        lax.fori_loop(0, (hi - lo) // 2, two_rows, 0)

    def residual(x, y, here, total):
        fb[x, y] = at_row(scale, x, y) * (total - at_row(diag, x, y) * here)

    for copy in copies[len(planes) : -1]:
        copy.wait()
    copies[-1].start()
    sweep(DEEP - 1, fa, residual)
    marks_copy.wait()
    copies[-1].wait()

    def add_sources(x, carry):
        for which in range(3):

            @pl.when(marked_s[which, x, CONTACT] + marked_s[which, x, CONTACT + 1] > 0)
            def _():
                face = faces[x, which]
                start = (1, DEEP, DEEP + BLK)[which]
                stop = (DEEP, DEEP + BLK, EXT - 1)[which]
                for y in range(start, stop):
                    spot = (y + YOFF, y - DEEP, y - DEEP - BLK)[which]
                    source = jnp.where(
                        first_lane,
                        pltpu.roll(face, (NZ - spot) % NZ, 1),
                        jnp.where(
                            last_lane, pltpu.roll(face, NZ - 1 - UPPER - spot, 1), 0.0
                        ),
                    )
                    fb[x, y] = fb[x, y] + at_row(scale, x, y) * source

        return carry

    lax.fori_loop(1, EXT - 1, add_sources, 0)

    def rescale(x, carry):
        here = scale[x]
        cx[x] = cx[x] * here * scale[jnp.minimum(x + 1, EXT - 1)]
        cy[x] = cy[x] * here * pltpu.roll(here, ROWS - 1, 0)
        cz[x] = cz[x] * here * pltpu.roll(here, NZ - 1, 1)
        return carry

    lax.fori_loop(0, EXT, rescale, 0)

    def mixed(dst, base, factor):
        def finish(x, y, here, total):
            dst[x, y] = factor * base[x, y] + total

        return finish

    def mapped(dst):
        def finish(x, y, here, total):
            dst[x, y] = here - total

        return finish

    def smooth(radius, base, one, two):
        sweep(radius + 2, base, mixed(one, base, MIX[0]))
        sweep(radius + 1, one, mixed(two, base, MIX[1]))
        sweep(radius, two, mixed(one, base, MIX[2]))

    smooth(5, fb, fa, fc)
    sweep(4, fa, mapped(fc))
    gram_first = gram(fa, (fb, fc), DEEP)

    def save(x, carry):
        for y in range(BLK):
            ub[x, y] = fa[DEEP + x, DEEP + y]
        return carry

    lax.fori_loop(0, BLK, save, 0)
    copy_u = pltpu.make_async_copy(ub, out_u, out_sems.at[0])
    copy_u.start()
    smooth(1, fc, fb, fa)
    copy_z = pltpu.make_async_copy(fb.at[mid, mid], out_z, out_sems.at[1])
    copy_z.start()
    sweep(0, fb, mapped(fa))
    gram_second = gram(fb, (fc, fa), DEEP)

    def save_scale(x, carry):
        out_scale[x] = scale[DEEP + x, BLK : 2 * BLK]
        return carry

    lax.fori_loop(0, BLK, save_scale, 0)

    volt[...] = jnp.zeros_like(volt)
    elane = lax.broadcasted_iota(jnp.int32, (PATS, ELECTRODES), 1)
    half = BLK // PATCH

    def electrode(i, carry):
        mark = marks[i]

        @pl.when(mark > 0)
        def _():
            face = i // (half * half)
            x0 = (i // half) % half * PATCH
            y0 = i % half * PATCH
            wanted = lane == face * (NZ - 1)
            sums = [zero, zero, zero]
            for dx in range(PATCH):
                for dy in range(PATCH):
                    x, y = x0 + dx, y0 + dy
                    weight = out_scale[x, pl.ds(y, 1), :]
                    sums[0] += own[x, y]
                    sums[1] += weight * ub[x, y]
                    sums[2] += weight * fb[DEEP + x, DEEP + y]
            for f in range(3):
                total = jnp.sum(jnp.where(wanted, sums[f], 0.0), axis=1, keepdims=True)
                volt[f] = volt[f] + jnp.where(elane == mark - 1, total, 0.0)

        return carry

    lax.fori_loop(0, 2 * half * half, electrode, 0)

    per = ELECTRODES // 8
    empty = jnp.zeros((PATS, 3 * per), F32)
    grams = jnp.concatenate([empty, gram_first], axis=1)
    rest = jnp.concatenate(
        [gram_second[:8], gram_second[8:], jnp.zeros((8, NZ - 4 * PATS), F32)], axis=1
    )
    for d in range(8):
        tile, spot = d * per // NZ, d * per % NZ
        picked = grams
        for f in range(3):
            part = volt[f, :, tile * NZ : (tile + 1) * NZ]
            part = pltpu.roll(part, (per * f - spot) % NZ, 1)
            inside = (lane >= per * f) & (lane < per * (f + 1))
            picked = jnp.where(inside, part, picked)
        for copy in range(out_chunk.shape[0]):
            out_chunk[copy, d, 0:PATS] = picked
            out_chunk[copy, d, PATS:] = rest
    copy_u.wait()
    copy_z.wait()


def main_call(side, marks, block, low, high, mate, away, cmate, caway):
    shape = jax.ShapeDtypeStruct
    field = pltpu.VMEM((EXT, EXT, PATS, NZ), F32)
    plane = pltpu.VMEM((EXT, ROWS, NZ), F32)
    return pl.pallas_call(
        main_kernel,
        out_shape=(
            shape((BLK, BLK, PATS, NZ), F32),
            shape((BLK, BLK, PATS, NZ), F32),
            shape((BLK, BLK, NZ), F32),
            shape((4, 8, PATS + 8, NZ), F32),
        ),
        in_specs=[SM, SM] + [HB] * 5 + [VM] * 2,
        out_specs=(HB, HB, VM, VM),
        scratch_shapes=[
            pltpu.VMEM((BLK, BLK, PATS, NZ), F32),
            pltpu.VMEM((BLK, BLK, PATS, NZ), F32),
            field, field, field,
            pltpu.VMEM((EXT, PATS, NZ), F32),
            pltpu.VMEM((EXT, PATS, NZ), F32),
            pltpu.VMEM((EXT, 3, PATS, NZ), F32),
            plane, plane, plane, plane, plane, plane,
            pltpu.VMEM((3, PATS, ELECTRODES), F32),
            pltpu.VMEM((3, MARKROWS, NZ), F32),
            pltpu.SMEM((3, MARKROWS, NZ), F32),
            pltpu.SemaphoreType.DMA,
            pltpu.SemaphoreType.DMA((16,)),
            pltpu.SemaphoreType.DMA((2,)),
        ],
        compiler_params=vmem(60),
    )(side, marks, block, low, high, mate, away, cmate, caway)


def solve_kernel(parts, out_mix, out_volt):
    volts = parts[0, 0:PATS]
    rest = parts[0, PATS:]
    for i in range(1, parts.shape[0]):
        volts = volts + parts[i, 0:PATS]
        rest = rest + parts[i, PATS:]
    lane = lax.broadcasted_iota(jnp.int32, (PATS, NZ), 1)
    second = jnp.concatenate([rest, pltpu.roll(rest, NZ - 2 * PATS, 1)], axis=0)

    a_at, b_at = (volts, NZ - 2 * PATS), (volts, NZ - PATS)
    c_at, e_at = (second, 0), (second, PATS)

    def move(source, target):
        return pltpu.roll(source[0], (target - source[1]) % NZ, 1)

    def pick(first, second, third):
        return jnp.where(
            lane < PATS,
            move(first, 0),
            jnp.where(
                lane < 2 * PATS,
                move(second, PATS),
                jnp.where(lane < 3 * PATS, move(third, 2 * PATS), 0.0),
            ),
        )

    table = jnp.concatenate([pick(b_at, c_at, a_at), pick(c_at, e_at, b_at)], axis=0)
    rows = lax.broadcasted_iota(jnp.int32, (2 * PATS, NZ), 0)
    for k in range(2 * PATS):
        pivot = table[k : k + 1] / table[k : k + 1, k : k + 1]
        table = jnp.where(rows == k, pivot, table - table[:, k : k + 1] * pivot)
    mix = table[:, 2 * PATS : 3 * PATS]
    eye = (
        lax.broadcasted_iota(jnp.int32, (PATS, PATS), 0)
        == lax.broadcasted_iota(jnp.int32, (PATS, PATS), 1)
    ).astype(F32)
    turned = lax.dot_general(
        eye, mix, (((1,), (1,)), ((), ())), precision=HIGHEST, preferred_element_type=F32
    )
    out_mix[...] = turned
    per = ELECTRODES // 8
    fields = jnp.concatenate(
        [pltpu.roll(volts, NZ - per, 1), pltpu.roll(volts, NZ - 2 * per, 1)], axis=0
    )
    total = volts + jnp.dot(turned, fields, precision=HIGHEST, preferred_element_type=F32)
    out_volt[...] = total * (1.0 / (PATCH * PATCH))


def solve_small(parts):
    shape = jax.ShapeDtypeStruct
    return pl.pallas_call(
        solve_kernel,
        out_shape=(shape((PATS, 2 * PATS), F32), shape((PATS, NZ), F32)),
        in_specs=[VM],
        out_specs=(VM, VM),
        compiler_params=vmem(60),
    )(parts)


PARTS = 4


def update_kernel(
    mix, scale, start_h, u_h, z_h, out_h, start, u, z, out, in_sems, out_sems
):
    count = BLK // PARTS
    reads, writes = [], []
    for n in range(PARTS):
        xs = pl.ds(n * count, count)
        pairs = ((u_h.at[xs], u.at[xs]), (z_h.at[xs], z.at[xs]), (start_h.at[:, xs], start.at[:, xs]))
        reads.append(
            [
                pltpu.make_async_copy(src, dst, in_sems.at[3 * n + m])
                for m, (src, dst) in enumerate(pairs)
            ]
        )
        writes.append(pltpu.make_async_copy(out.at[:, xs], out_h.at[:, xs], out_sems.at[n]))
        for copy in reads[n]:
            copy.start()
    left = jnp.concatenate(
        [jnp.concatenate([part] * 3, axis=1) for part in split3(mix[...])], axis=0
    )

    def row(x, carry):
        data = jnp.concatenate(
            [
                jnp.concatenate([field[x, y] for y in range(BLK)], axis=1)
                for field in (u, z)
            ],
            axis=0,
        )
        right = jnp.concatenate(split3(data), axis=0)
        both = jnp.dot(left, right, preferred_element_type=F32)
        both = both[:PATS] + (both[PATS : 2 * PATS] + both[2 * PATS :])
        change = jnp.stack(
            [
                both[:, y * NZ : (y + 1) * NZ] * scale[x, pl.ds(y, 1), :]
                for y in range(BLK)
            ],
            axis=0,
        )
        out[:, x] = start[:, x] + pltpu.einshape("ypz->pyz", change)
        return carry

    for n in range(PARTS):
        for copy in reads[n]:
            copy.wait()
        lax.fori_loop(n * count, (n + 1) * count, row, 0)
        writes[n].start()
    for copy in writes:
        copy.wait()


def update(mix, start, u, z, scale):
    block = pltpu.VMEM((BLK, BLK, PATS, NZ), F32)
    return pl.pallas_call(
        update_kernel,
        out_shape=jax.ShapeDtypeStruct(start.shape, F32),
        in_specs=[VM, VM, HB, HB, HB],
        out_specs=HB,
        scratch_shapes=[
            pltpu.VMEM((PATS, BLK, BLK, NZ), F32), block, block,
            pltpu.VMEM((PATS, BLK, BLK, NZ), F32),
            pltpu.SemaphoreType.DMA((3 * PARTS,)),
            pltpu.SemaphoreType.DMA((PARTS,)),
        ],
        compiler_params=vmem(60),
    )(mix, scale, start, u, z)


def face_blocks(electrode_map, currents, contact_gain):
    numbers = jnp.arange(1, ELECTRODES + 1, dtype=jnp.int32)
    onehot = (electrode_map[..., None] == numbers).astype(F32)
    contact = jnp.einsum("fxye,e->xyf", onehot, contact_gain, precision=HIGHEST)
    source = jnp.einsum("fxye,ep->fxpy", onehot, currents, precision=HIGHEST)
    gap = lambda width: jnp.zeros((BLK, PATS, width), F32)
    return jnp.concatenate(
        [
            source[0], gap(CONTACT - BLK), contact, gap(UPPER - CONTACT - 2),
            source[1], gap(NZ - UPPER - BLK),
        ],
        axis=2,
    )


def body(start_field, currents, electrode_map, contact_gain, region_label, region_cond, texture):
    gx, gy = lax.axis_size(GX), lax.axis_size(GY)
    side = lax.axis_index("c").astype(jnp.int32).reshape(1)
    marks = electrode_map[:, ::PATCH, ::PATCH].reshape(-1)
    face = face_blocks(electrode_map, currents, contact_gain)
    block, up, down, mate, away = pack(
        side, region_cond, start_field, region_label, texture, face
    )
    rise = [(i, i + 1) for i in range(gx - 1)]
    fall = [(j, i) for i, j in rise]
    pairs = [(i, i + 1) for i in range(0, gy, 2)]
    gaps = [(i, i + 1) for i in range(1, gy - 1, 2)]
    within = pairs + [(j, i) for i, j in pairs]
    across = gaps + [(j, i) for i, j in gaps]
    low = lax.ppermute(up, GX, rise)
    high = lax.ppermute(down, GX, fall)
    away = lax.ppermute(away, GY, across)
    mate = lax.ppermute(mate, GY, within)
    cmate, caway = corners(side, low, high)
    caway = lax.ppermute(caway, GY, across)
    cmate = lax.ppermute(cmate, GY, within)
    u, z, scale, chunk = main_call(
        side, marks, block, low, high, mate, away, cmate, caway
    )
    nz = lax.axis_size("z")
    parts = chunk.reshape((-1,) + chunk.shape[2:])
    parts = lax.all_to_all(parts, ("x", "y", "c"), 0, 0, tiled=True)
    chunk = jnp.sum(parts, axis=0)
    parts = jnp.broadcast_to(chunk[None], (nz,) + chunk.shape)
    parts = lax.all_to_all(parts, "z", 0, 0, tiled=True)
    mix, volt = solve_small(parts)
    volts = jnp.broadcast_to(volt[None], (gy,) + volt.shape)
    volts = lax.all_to_all(volts, GY, 0, 0, tiled=True)
    result = update(mix, start_field, u, z, scale)
    per = ELECTRODES // gy
    voltages = volts[:, :, :per].transpose(1, 0, 2).reshape(PATS, ELECTRODES)
    return result, voltages


def solution(mesh):
    torus = Mesh(mesh.devices.reshape(8, 4, 4, 2), GX + GY)
    placed = (
        P(None, GX, GY, None),
        P(),
        P(None, GX, GY),
        P(),
        P(GX, GY, None),
        P(),
        P(GX, GY, None),
    )
    return jax.shard_map(
        body,
        mesh=torus,
        in_specs=placed,
        out_specs=(P(None, GX, GY, None), P()),
        check_vma=False,
    )
```
